256 devices in a mesh: section: 16 (over y, x), dp: 16 (over z, core).
Axes of the slice: x: 4, y: 4, z: 8, core: 2. Of those that a mesh axis runs over, the one named last changes fastest.
Arguments:
- acts: bfloat16 [16, 1, 2048, 4608], P('section', None, 'dp'), may hold values from -6 to 6
- output_gradient: bfloat16 [1, 2048, 4608], P(None, 'dp'), may hold values from -6 to 6
- gains: float32 [16, 4608], P('section'), may hold values from 0.5 to 1.5
- adapter_down_weight: bfloat16 [16, 4608, 128], P('section'), may hold values from -0.5 to 0.5
- adapter_up_weight: bfloat16 [16, 4608, 128], P('section'), may hold values from -0.5 to 0.5
- thresholds: float32 [16, 1, 64], P('section'), may hold values from 10 to 40
- document_lengths: int32 [1, 64], replicated, may hold values from 1 to 64, 2048 in all within a row
- owners: int32 [1, 64], replicated, may hold values from 0 to 15, as said below
Outputs:
- input_grads: bfloat16 [16, 1, 2048, 4608], P('section', None, 'dp')
- lora_grad: float32 [16, 4608, 256], P('section', 'dp')
- owned_ratios: float32 [16, 1, 128], P('section', None, 'dp')
The draws below stay inside these ranges and needn't reach their ends.
Inputs may be any that keep to these rules, and one draw needn't show every extreme that they name: `document_lengths`: each row sums to 2048; its longest document has exactly 64 tokens. `owners`: in each row no device owns more than 8 documents, and some device owns exactly 8.
All inputs are finite; a program needn't handle non-finite values.
Results may differ from the reference program's by a relative error of at most 0.019.
Values may be sent and summed in bfloat16 or wider, within the bound.
A program may use at most 64 MiB of HBM per device.

```python
import math
import jax
import jax.numpy as jnp
import numpy as np
from jax import lax

MODEL_WIDTH = 4608
ADAPTER_RANK = 128
TOK_DEV = 128
MICRO_BATCHES = 1
OWN = 8
MOST = 64
SEQ = 2048
PACKED_DOCUMENTS = 64
WINDOW_LAYERS = 16
N_DP = 16


def shared_direction(key):
    flips = jax.random.bernoulli(jax.random.fold_in(key, 101), 0.5, (MODEL_WIDTH,))
    return jnp.where(flips, 1.0, -1.0).astype(jnp.float32)


def mixed_field(noise, common_key, common_scale, along, direction):
    common_shape = noise.shape[:-2] + (1, MODEL_WIDTH)
    common = jnp.clip(jax.random.normal(common_key, common_shape, jnp.float32), -4.0, 4.0) * common_scale
    values = noise + common + along * direction
    return jnp.clip(values, -6.0, 6.0)


def adapter_matrix(key, direction):
    base_key, column_key, sign_key = jax.random.split(key, 3)
    spread = MODEL_WIDTH ** (-0.5)
    base = jnp.clip(jax.random.normal(base_key, (WINDOW_LAYERS, MODEL_WIDTH, ADAPTER_RANK), jnp.float32), -4.0, 4.0) * spread
    column = jnp.clip(jax.random.normal(column_key, (WINDOW_LAYERS, MODEL_WIDTH), jnp.float32), -4.0, 4.0) * (0.25 * spread)
    signs = jnp.where(jax.random.bernoulli(sign_key, 0.5, (WINDOW_LAYERS, 1)), 1.0, -1.0).astype(jnp.float32)
    first = signs * (0.46 * spread) * direction[None, :] + column
    return base.at[:, :, 0].set(first)


def draw_acts(key, part):
    direction = shared_direction(key)
    key = jax.random.fold_in(key, 11)
    noise_key, common_key, along_key = jax.random.split(key, 3)
    shape = (WINDOW_LAYERS, MICRO_BATCHES, SEQ, MODEL_WIDTH)
    along_shape = (WINDOW_LAYERS, MICRO_BATCHES, SEQ, 1)
    noise = jnp.clip(jax.random.normal(noise_key, shape, jnp.float32), -3.0, 3.0)
    along = jnp.clip(jax.random.normal(along_key, along_shape, jnp.float32), -2.5, 2.5) * 0.8
    values = mixed_field(noise, common_key, 0.33, along, direction)
    return values.astype(jnp.bfloat16)


def draw_output_gradient(key, part):
    direction = shared_direction(key)
    key = jax.random.fold_in(key, 13)
    noise_key, common_key, along_key = jax.random.split(key, 3)
    shape = (MICRO_BATCHES, SEQ, MODEL_WIDTH)
    along_shape = (MICRO_BATCHES, SEQ, 1)
    noise = jnp.clip(jax.random.normal(noise_key, shape, jnp.float32), -3.0, 3.0)
    along = jnp.clip(jax.random.normal(along_key, along_shape, jnp.float32), -2.5, 2.5) * 0.8
    values = mixed_field(noise, common_key, 0.33, along, direction)
    return values.astype(jnp.bfloat16)


def draw_adapter_down_weight(key, part):
    direction = shared_direction(key)
    key = jax.random.fold_in(key, 17)
    return adapter_matrix(key, direction).astype(jnp.bfloat16)


def draw_adapter_up_weight(key, part):
    direction = shared_direction(key)
    key = jax.random.fold_in(key, 19)
    return adapter_matrix(key, direction).astype(jnp.bfloat16)


def draw_owners(key, part):
    key = jax.random.fold_in(key, 7)

    def one_row(row_key):
        first_key, second_key, third_key = jax.random.split(row_key, 3)
        slot_total = 2 * PACKED_DOCUMENTS
        slot_owner = jnp.arange(slot_total, dtype=jnp.int32) // OWN
        favored = jax.random.randint(first_key, (), 0, slot_total // OWN, dtype=jnp.int32)
        order_keys = jax.random.permutation(second_key, slot_total).astype(jnp.int32)
        scores = jnp.where(slot_owner == favored, order_keys - slot_total, order_keys)
        chosen = slot_owner[jnp.argsort(scores, stable=True)][:PACKED_DOCUMENTS]
        return chosen[jax.random.permutation(third_key, PACKED_DOCUMENTS)]
    return jax.vmap(one_row)(jax.random.split(key, MICRO_BATCHES))


def steps_of(key, shape, cuts, least, largest):
    def one(dim, shards_of):
        heights = jax.random.uniform(jax.random.fold_in(jax.random.fold_in(key, 6), dim), (shards_of,), jnp.float32, least / len(cuts), largest / len(cuts))
        return jnp.repeat(jnp.exp(heights), shape[dim] // shards_of).reshape((-1,) + (1,) * (len(shape) - dim - 1))

    level = one(*cuts[0])
    for cut in cuts[1:]:
        level = level * one(*cut)
    return level


def profile(number_of, total, most, lean):
    portions = [(1 << 20) // math.isqrt(standing ** lean) + 1 for standing in range(2, number_of + 1)]
    rest, counts = total - most - (number_of - 1), [1] * (number_of - 1)
    while rest > 0:
        free = [i for i in range(number_of - 1) if counts[i] < most]
        whole, budget = sum([portions[i] for i in free]), rest
        for i in free:
            more = min(most - counts[i], max(1, budget * portions[i] // whole), rest)
            counts[i] = counts[i] + more
            rest = rest - more
    return np.array([most] + counts)


def uneven(own_key, count, total, limit, slope):
    if count == 2:
        one = jax.random.randint(own_key, (), max(1, total - limit), min(limit, total - 1) + 1)
        return jnp.stack([one, total - one])
    lengths = jnp.asarray(profile(count, total, limit, slope), jnp.int32)
    pairs = (count - 1) // 2
    source_of, sink = lengths[1:1 + 2 * pairs:2], lengths[2:2 + 2 * pairs:2]
    room = jnp.minimum(source_of - 1, limit - sink)
    moved = jax.random.randint(jax.random.fold_in(own_key, 1), (pairs,), 0, 1 << 20) % (room + 1)
    lengths = lengths.at[1:1 + 2 * pairs:2].set(source_of - moved).at[2:2 + 2 * pairs:2].set(sink + moved)
    return lengths[jax.random.permutation(jax.random.fold_in(own_key, 2), count)]


def setup_inputs(seed: int = 0) -> dict:
    splits = jax.random.split(jax.random.key(seed), 9)
    acts = draw_acts(jax.random.fold_in(splits[8], 71), 0)
    output_gradient = draw_output_gradient(jax.random.fold_in(splits[8], 71), 0)
    gains = jnp.clip(1.0 + 0.1 * jax.random.normal(splits[2], (WINDOW_LAYERS, MODEL_WIDTH), jnp.float32), 0.5, 1.5)
    adapter_down_weight = draw_adapter_down_weight(jax.random.fold_in(splits[8], 71), 0)
    adapter_up_weight = draw_adapter_up_weight(jax.random.fold_in(splits[8], 71), 0)
    thresholds = jnp.clip(jnp.exp(math.log(40.0) - 1.3862944 * jax.random.uniform(splits[5], (WINDOW_LAYERS, MICRO_BATCHES, PACKED_DOCUMENTS), jnp.float32) ** steps_of(splits[5], (WINDOW_LAYERS, MICRO_BATCHES, PACKED_DOCUMENTS), ((0, 16),), -0.2, 0.2)), 10.0, 40.0)
    document_lengths = jax.vmap(lambda own: uneven(own, PACKED_DOCUMENTS, SEQ, MOST, 1))(jax.random.split(splits[6], MICRO_BATCHES)).reshape((MICRO_BATCHES, PACKED_DOCUMENTS)).astype(jnp.int32)
    owners = draw_owners(jax.random.fold_in(splits[8], 71), 0)
    return dict(acts=acts, output_gradient=output_gradient, gains=gains, adapter_down_weight=adapter_down_weight, adapter_up_weight=adapter_up_weight, thresholds=thresholds, document_lengths=document_lengths, owners=owners)


NORM_EPS = 1e-06
HIGHEST_PRECISION = lax.Precision.HIGHEST

def doc_table(document_lengths):
    seq_ends = jnp.cumsum(document_lengths, axis=1).astype(jnp.int32)
    seq_pos = jnp.arange(SEQ, dtype=jnp.int32)
    return lax.optimization_barrier(jnp.sum((seq_ends[:, None, :] <= seq_pos[None, :, None]).astype(jnp.int32), axis=2))

def with_next(blocks, filler):
    tail_rows = blocks[:, 1:, :MOST]
    pad_block = jnp.zeros_like(blocks[:, :1, :MOST]) + filler
    return jnp.concatenate([blocks, jnp.concatenate([tail_rows, pad_block], axis=1)], axis=2)

def as_blocks(values):
    return values.reshape(MICRO_BATCHES, N_DP, TOK_DEV, values.shape[-1])

def block_gram(values):
    blocks = as_blocks(values).astype(jnp.float32)
    columns = with_next(blocks, 0.0)
    return jnp.einsum('mbtf,mbsf->mbts', blocks, columns)

def pair_rows(normalized_input, low_rank, hidden, incoming_gradient, doc_of):
    kernel = block_gram(normalized_input) * block_gram(low_rank) + block_gram(hidden) * block_gram(incoming_gradient)
    doc_rows = doc_of.reshape(MICRO_BATCHES, N_DP, TOK_DEV)
    doc_cols = with_next(doc_rows[..., None], PACKED_DOCUMENTS)[..., 0]
    column_weight = jnp.where(jnp.arange(TOK_DEV + MOST, dtype=jnp.int32) < TOK_DEV, 1.0, 2.0).astype(jnp.float32)
    weight = jnp.where(doc_rows[..., :, None] == doc_cols[..., None, :], column_weight, 0.0)
    return lax.optimization_barrier(jnp.sum(kernel * weight, axis=3)).reshape(MICRO_BATCHES, SEQ)

def owner_table(ratio, owners):
    owner_ids = jnp.arange(N_DP, dtype=jnp.int32)
    mine = (owners[:, None, :] == owner_ids[None, :, None]).astype(jnp.int32)
    rank_of = jnp.cumsum(mine, axis=2).astype(jnp.int32) - 1
    slot_ids = jnp.arange(OWN, dtype=jnp.int32)
    picked = jnp.where((mine[..., None] == 1) & (rank_of[..., None] == slot_ids), 1.0, 0.0).astype(jnp.float32)
    table = jnp.einsum('mk,mnkj->mnj', ratio, picked, precision=HIGHEST_PRECISION)
    return table.reshape(MICRO_BATCHES, N_DP * OWN)

def reference(acts, output_gradient, gains, adapter_down_weight, adapter_up_weight, thresholds, document_lengths, owners):
    doc_of = doc_table(document_lengths)
    doc_ids = jnp.arange(PACKED_DOCUMENTS, dtype=jnp.int32)
    one_hot = (doc_of[:, :, None] == doc_ids[None, None, :]).astype(jnp.float32)
    incoming_gradient = output_gradient
    gradient_stack, adapter_stack, held_layers = ([], [], [])
    for section_position in reversed(range(WINDOW_LAYERS)):
        layer_inputs = acts[section_position].astype(jnp.float32)
        norm_gain = gains[section_position]
        down_matrix = adapter_down_weight[section_position].astype(jnp.float32)
        up_matrix = adapter_up_weight[section_position].astype(jnp.float32)
        clip_scale = lax.rsqrt(lax.optimization_barrier(jnp.mean(layer_inputs * layer_inputs, axis=-1, keepdims=True)) + NORM_EPS)
        centered_input = layer_inputs * clip_scale
        low_rank = jnp.einsum('mtd,dr->mtr', incoming_gradient.astype(jnp.float32), up_matrix).astype(jnp.bfloat16)
        back = jnp.einsum('mtr,dr->mtd', low_rank.astype(jnp.float32), down_matrix)
        scaled_gradient = back * norm_gain
        final_result = incoming_gradient.astype(jnp.float32) + clip_scale * (scaled_gradient - centered_input * lax.optimization_barrier(jnp.mean(scaled_gradient * centered_input, axis=-1, keepdims=True)))
        final_result = final_result.astype(jnp.bfloat16)
        normalized_input = (centered_input * norm_gain).astype(jnp.bfloat16)
        hidden = jnp.einsum('mtd,dr->mtr', normalized_input.astype(jnp.float32), down_matrix).astype(jnp.bfloat16)
        row_sums = pair_rows(normalized_input, low_rank, hidden, incoming_gradient, doc_of)
        pair_sum = jnp.einsum('mt,mtk->mk', row_sums, one_hot, precision=HIGHEST_PRECISION)
        ratio = jnp.sqrt(pair_sum / (MODEL_WIDTH * ADAPTER_RANK) + NORM_EPS) / thresholds[section_position]
        clip_bound = jnp.minimum(1.0, 1.0 / ratio)
        token_clip = jnp.einsum('mtk,mk->mt', one_hot, clip_bound, precision=HIGHEST_PRECISION)
        weighted_low = (token_clip[..., None] * low_rank.astype(jnp.float32)).astype(jnp.bfloat16)
        weighted_hidden = (token_clip[..., None] * hidden.astype(jnp.float32)).astype(jnp.bfloat16)
        down_gradient = jnp.einsum('mtd,mtr->dr', normalized_input.astype(jnp.float32), weighted_low.astype(jnp.float32))
        up_gradient = jnp.einsum('mtd,mtr->dr', incoming_gradient.astype(jnp.float32), weighted_hidden.astype(jnp.float32))
        adapter_stack.append(jnp.concatenate([down_gradient, up_gradient], axis=1) / (MICRO_BATCHES * PACKED_DOCUMENTS))
        held_layers.append(owner_table(ratio, owners))
        gradient_stack.append(final_result)
        incoming_gradient = final_result
    return (jnp.stack(gradient_stack[::-1]), jnp.stack(adapter_stack[::-1]), jnp.stack(held_layers[::-1]))
```

```python
import functools

import jax
import jax.numpy as jnp
from jax import lax
from jax.experimental import pallas as pl
from jax.experimental.pallas import tpu as pltpu
from jax.sharding import PartitionSpec as P

OWN = 8
NORM_EPS = 1e-06
MESH = pl.DeviceIdType.MESH
F32, BF16 = jnp.float32, jnp.bfloat16
R = 8
G = 16
LANE = 128
CHUNKS = 3


def dot(a, b):
    return jnp.dot(a, b, preferred_element_type=F32)


def dot_nt(a, b):
    return lax.dot_general(a, b, (((1,), (1,)), ((), ())), preferred_element_type=F32)


def halves(v, half):
    return jnp.concatenate([v[:, :half], v[:, half:]], axis=0)


def kernel(n_sec, n_dp, *refs):
    (acts, og, gains, dn, up, thr, lens, own, ig, lora, owned,
     xv, flat, ucat, dv, dtc, normed, xp, arr, outp, outf, scale, hidf, hidb, lowf, lowb,
     r_n, r_a, r_l, r_h, nw, hw, parts, part_f, other, lora_v, hid_t, low_t, doc_row, doc_col,
     s_load, s_out, s_chain, c_send, rs, rso, ss, sso, p_send, p_recv, o_send, o_recv) = refs
    tok, feat = xv.shape
    half = feat // 2
    n_docs = lens.shape[1]
    pieces, groups = tok // R, tok // G
    n_z = n_dp // 2
    per_chip = feat // n_z
    win = r_n.shape[1]
    blocks = n_dp // 2
    span = blocks * tok
    cols = tok + tok // 2
    lanes = half // CHUNKS

    sec = lax.axis_index("section")
    me = lax.axis_index("dp")
    z, core = me // 2, lax.rem(me, 2)
    side = me // blocks
    slot = lax.rem(me, blocks)
    last = n_sec - 1
    first_half = core == 0

    def load(src, dst, i):
        return pltpu.make_async_copy(src, dst, s_load.at[i])

    loads = [
        load(acts, xv, 0),
        load(dn, dv, 1),
        load(up.at[pl.ds(0, half)], ucat.at[:, pl.ds(0, LANE)], 2),
        load(up.at[pl.ds(half, half)], ucat.at[:, pl.ds(LANE, LANE)], 3),
    ]
    for c in loads:
        c.start()

    @pl.when(sec == last)
    def _():
        load(og, flat, 4).start()

    barrier = pltpu.get_barrier_semaphore()

    def greet(who):
        pl.semaphore_signal(barrier, inc=1, device_id=who, device_id_type=MESH)

    @pl.when(sec > 0)
    def _():
        greet({"section": sec - 1})

    @pl.when(sec < last)
    def _():
        greet({"section": sec + 1})

    for peer in range(n_dp):
        @pl.when(me != peer)
        def _():
            greet({"dp": peer})

    @pl.when(core == 1)
    def _():
        for r in (r_n, r_a, r_l, r_h):
            r[pl.ds(span, tok // 2), :] = jnp.zeros((tok // 2, r.shape[1]), BF16)

    loads[0].wait()

    def norm_group(q, _):
        rows = pl.ds(pl.multiple_of(q * G, G), G)
        v = xv[rows, :].astype(F32)
        s = lax.rsqrt(jnp.sum(v * v, axis=1, keepdims=True) / feat + NORM_EPS)
        scale[rows, :] = jnp.broadcast_to(s, (G, LANE))
        normed[rows, :] = (v * s * gains[...]).astype(BF16)
        xp[2 * q] = halves(v[:R], half).astype(BF16)
        xp[2 * q + 1] = halves(v[R:], half).astype(BF16)
        return 0

    lax.fori_loop(0, groups, norm_group, 0)
    loads[1].wait()
    hidf[...] = jnp.zeros_like(hidf)

    def down_tile(t, _):
        here = pl.ds(pl.multiple_of(t * LANE, LANE), LANE)
        there = pl.ds(pl.multiple_of(t * LANE + half, LANE), LANE)
        dtc[pl.ds(0, LANE), here] = (dv[here, :].astype(F32).T * gains[:, here]).astype(BF16)
        dtc[pl.ds(LANE, LANE), here] = (dv[there, :].astype(F32).T * gains[:, there]).astype(BF16)
        hidf[...] += dot(normed[:, here], dv[here, :]) + dot(normed[:, there], dv[there, :])
        return 0

    lax.fori_loop(0, half // LANE, down_tile, 0)
    hidb[...] = hidf[...].astype(BF16)

    @pl.when(sec == last)
    def _():
        load(og, flat, 4).wait()

        def pack(q, _):
            rows = pl.ds(pl.multiple_of(q * G, G), G)
            v = flat[rows, :].astype(F32)
            arr[2 * q] = halves(v[:R], half).astype(BF16)
            arr[2 * q + 1] = halves(v[R:], half).astype(BF16)
            return 0

        lax.fori_loop(0, groups, pack, 0)

    loads[2].wait()
    loads[3].wait()

    ends = jnp.where(sec > 0, 1, 0) + jnp.where(sec < last, 1, 0)
    pl.semaphore_wait(barrier, n_dp - 1 + ends)

    def spread(src, dst, i, row, n, window):
        for zz in range(n_z):
            start = per_chip * zz // LANE * LANE if window else 0
            width = win if window else LANE
            s = src.at[pl.ds(row, n), pl.ds(start, width)]

            def to(dest_core, at, send, recv):
                d = dst.at[pl.ds(at, n), :]
                dest = 2 * zz + dest_core

                @pl.when(dest == me)
                def _():
                    pltpu.make_async_copy(s, d, recv.at[i]).start()

                @pl.when(dest != me)
                def _():
                    pltpu.make_async_remote_copy(
                        src_ref=s, dst_ref=d, send_sem=send.at[i], recv_sem=recv.at[i],
                        device_id={"dp": dest}, device_id_type=MESH,
                    ).start()

            to(side, pl.multiple_of(slot * tok + row, G), ss, rs)

            @pl.when((me == blocks) & (row < tok // 2))
            def _():
                to(0, pl.multiple_of(span + lax.rem(row, tok // 2), G), sso, rso)

    def spread_own():
        def group(q, _):
            row = pl.multiple_of(q * G, G)
            spread(normed, r_n, 0, row, G, True)
            spread(hidb, r_h, 1, row, G, False)
            return 0

        lax.fori_loop(0, groups, group, 0)

    def doc_tables():
        k_row = lax.broadcasted_iota(jnp.int32, (n_docs, n_docs), 1)
        k_col = lax.broadcasted_iota(jnp.int32, (n_docs, n_docs), 0)
        len_row = lens[...].astype(F32)
        len_col = jnp.sum(jnp.where(k_row == k_col, len_row, 0.0), axis=1, keepdims=True)
        ends_col = jnp.sum(jnp.where(k_row <= k_col, len_row, 0.0), axis=1, keepdims=True)
        ends_row = jnp.sum(jnp.where(k_col <= k_row, len_col, 0.0), axis=0, keepdims=True)
        base = core * span

        def at(b, _):
            start = pl.multiple_of(b * tok, tok)
            pos_r = (lax.broadcasted_iota(jnp.int32, (n_docs, tok), 1) + (base + start)).astype(F32)
            doc_row[:, pl.ds(start, tok)] = jnp.broadcast_to(
                jnp.sum(jnp.where(ends_col <= pos_r, 1.0, 0.0), axis=0, keepdims=True), (8, tok))
            pos_c = (lax.broadcasted_iota(jnp.int32, (tok, n_docs), 0) + (base + start)).astype(F32)
            doc_col[pl.ds(start, tok), :] = jnp.broadcast_to(
                jnp.sum(jnp.where(ends_row <= pos_c, 1.0, 0.0), axis=1, keepdims=True), (tok, LANE))
            return 0

        lax.fori_loop(0, blocks + 1, at, 0)

    @pl.when(sec < n_sec // 2)
    def _():
        spread_own()

    def chain_copy(p, c):
        there = pl.ds(c * lanes, lanes)
        return pltpu.make_async_remote_copy(
            src_ref=outp.at[p, :, there], dst_ref=arr.at[p, :, there],
            send_sem=c_send, recv_sem=s_chain.at[p, c],
            device_id={"section": jnp.maximum(sec - 1, 0)}, device_id_type=MESH,
        )

    def piece(p):
        row = pl.multiple_of(p * R, R)
        rows = pl.ds(row, R)
        for c in range(CHUNKS):
            @pl.when(sec < last)
            def _():
                chain_copy(p, c).wait_recv()

        both = dot(arr[p], ucat[...])
        low = (both[:R, :LANE] + both[R:, LANE:]).astype(BF16).astype(F32)
        lowf[rows, :] = low
        s = scale[rows, :1]
        k = s * s * (jnp.sum(low * hidf[rows, :], axis=1, keepdims=True) / feat)
        zero = jnp.zeros_like(low)
        wide = jnp.concatenate(
            [jnp.concatenate([low, zero], axis=1), jnp.concatenate([zero, low], axis=1)], axis=0
        ).astype(BF16)
        s2, k2 = jnp.concatenate([s, s], axis=0), jnp.concatenate([k, k], axis=0)
        for c in range(CHUNKS):
            there = pl.ds(c * lanes, lanes)
            back = dot(wide, dtc[:, there])
            out = arr[p, :, there].astype(F32) + s2 * back - k2 * xp[p, :, there].astype(F32)
            outp[p, :, there] = out.astype(BF16)

            @pl.when(sec > 0)
            def _():
                chain_copy(p, c).start()

    def group(q, _):
        piece(2 * q)
        piece(2 * q + 1)
        row = pl.multiple_of(q * G, G)
        rows = pl.ds(row, G)

        def unpack(src):
            a, b = src[2 * q].astype(F32), src[2 * q + 1].astype(F32)
            return (jnp.concatenate([a[:R], b[:R]], axis=0).astype(BF16),
                    jnp.concatenate([a[R:], b[R:]], axis=0).astype(BF16))

        @pl.when(sec < last)
        def _():
            lo, hi = unpack(arr)
            flat[rows, pl.ds(0, half)] = lo
            flat[rows, pl.ds(half, half)] = hi

        lo, hi = unpack(outp)
        outf[rows, pl.ds(0, half)] = lo
        outf[rows, pl.ds(half, half)] = hi
        lowb[rows, :] = lowf[rows, :].astype(BF16)
        spread(flat, r_a, 2, row, G, True)
        spread(lowb, r_l, 3, row, G, False)
        pltpu.make_async_copy(outf.at[rows], ig.at[rows], s_out.at[0]).start()
        return 0

    lax.fori_loop(0, groups, group, 0)

    @pl.when(sec >= n_sec // 2)
    def _():
        spread_own()

    def arrived(dst, i):
        pltpu.make_async_copy(dst.at[pl.ds(0, span)], dst.at[pl.ds(0, span)], rs.at[i]).wait()

        @pl.when(first_half)
        def _():
            over = dst.at[pl.ds(span, tok // 2)]
            pltpu.make_async_copy(over, over, rso.at[i]).wait()

    doc_tables()
    arrived(r_n, 0)
    arrived(r_h, 1)
    offset = lax.rem(z, 2) * (LANE // 2)
    lane = lax.broadcasted_iota(jnp.int32, (1, win), 1)
    inside = jnp.where((lane >= offset) & (lane < offset + per_chip), 1.0, 0.0)
    column = jnp.where(lax.broadcasted_iota(jnp.int32, (1, cols), 1) < tok, 1.0, 2.0)

    def mine(src, b):
        return (src[pl.ds(b * tok, tok), :].astype(F32) * inside).astype(BF16)

    for b in range(blocks):
        there = pl.ds(b * tok, cols)
        same = doc_col[pl.ds(b * tok, tok), :1] == doc_row[:1, there]
        weight = jnp.where(same, column, 0.0)
        nw[b] = weight * dot_nt(mine(r_n, b), r_n[there, :])
        hw[b] = weight * dot_nt(r_h[pl.ds(b * tok, tok), :], r_h[there, :])
        hid_t[:, pl.ds(b * tok, tok)] = r_h[pl.ds(b * tok, tok), :].astype(F32).T

    arrived(r_l, 3)
    arrived(r_a, 2)
    total = jnp.zeros((1, LANE), F32)
    doc_lane = lax.broadcasted_iota(jnp.int32, (tok, LANE), 1).astype(F32)
    for b in range(blocks):
        there, here = pl.ds(b * tok, cols), pl.ds(b * tok, tok)
        pair = nw[b] * dot_nt(r_l[here, :], r_l[there, :]) + hw[b] * dot_nt(mine(r_a, b), r_a[there, :])
        row_sum = jnp.sum(pair, axis=1, keepdims=True)
        total += jnp.sum(jnp.where(doc_col[here, :] == doc_lane, row_sum, 0.0), axis=0, keepdims=True)
    parts[me] = jnp.broadcast_to(total, (8, LANE))

    for peer in range(n_dp):
        @pl.when(me != peer)
        def _():
            pltpu.make_async_remote_copy(
                src_ref=parts.at[me], dst_ref=parts.at[me], send_sem=p_send, recv_sem=p_recv,
                device_id={"dp": peer}, device_id_type=MESH,
            ).start()

    for b in range(blocks):
        here = pl.ds(b * tok, tok)
        low_t[:, here] = r_l[here, :].astype(F32).T

    most = parts.at[pl.ds(0, n_dp - 1)]
    pltpu.make_async_copy(most, most, p_recv).wait()
    pair_sum = jnp.sum(parts[...], axis=0)[:1, :n_docs]
    ratio = jnp.sqrt(pair_sum / (feat * LANE) + NORM_EPS) / thr[...]
    clip = jnp.minimum(1.0, 1.0 / ratio)
    k_row = lax.broadcasted_iota(jnp.int32, (n_docs, n_docs), 1)
    k_col = lax.broadcasted_iota(jnp.int32, (n_docs, n_docs), 0)
    clip_col = jnp.sum(jnp.where(k_row == k_col, clip, 0.0), axis=1, keepdims=True)
    doc_id = lax.broadcasted_iota(jnp.int32, (n_docs, span), 0).astype(F32)
    token_clip = jnp.sum(
        jnp.where(doc_row[:1, pl.ds(0, span)] == doc_id, clip_col, 0.0), axis=0, keepdims=True)
    down = dot((low_t[...] * token_clip).astype(BF16), r_n[pl.ds(0, span), :])
    up_g = dot((hid_t[...] * token_clip).astype(BF16), r_a[pl.ds(0, span), :])
    part_f[:, pl.ds(0, LANE)] = down.T
    part_f[:, pl.ds(LANE, LANE)] = up_g.T
    own_rows = pl.multiple_of(offset + core * (per_chip // 2), 8)
    far_rows = pl.multiple_of(offset + (1 - core) * (per_chip // 2), 8)
    swap = pltpu.make_async_remote_copy(
        src_ref=part_f.at[pl.ds(far_rows, per_chip // 2)], dst_ref=other,
        send_sem=o_send, recv_sem=o_recv,
        device_id={"dp": 2 * z + (1 - core)}, device_id_type=MESH,
    )
    swap.start()

    own_row = jnp.where(own[...] == me, 1.0, 0.0)
    own_col = jnp.sum(jnp.where(k_row == k_col, own_row, 0.0), axis=1, keepdims=True)
    rank_col = jnp.sum(jnp.where(k_row <= k_col, own_row, 0.0), axis=1, keepdims=True) - 1.0
    ratio_col = jnp.sum(jnp.where(k_row == k_col, ratio, 0.0), axis=1, keepdims=True)
    slot_id = lax.broadcasted_iota(jnp.int32, (n_docs, OWN), 1).astype(F32)
    held = jnp.where((own_col > 0.5) & (rank_col == slot_id), ratio_col, 0.0)
    owned[...] = jnp.sum(held, axis=0, keepdims=True)

    swap.wait()
    lora_v[...] = (part_f[pl.ds(own_rows, per_chip // 2), :] + other[...]) / n_docs
    store = pltpu.make_async_copy(lora_v, lora, s_out.at[1])
    store.start()

    pltpu.make_async_copy(most, most, p_send).wait()

    @pl.when(sec > 0)
    def _():
        pltpu.make_async_copy(outp, outp, c_send).wait()

    for i, dst in enumerate((r_n, r_h, r_a, r_l)):
        @pl.when(core == side)
        def _():
            whole = dst.at[pl.ds(0, (n_z - 1) * tok)]
            pltpu.make_async_copy(whole, whole, ss.at[i]).wait()

        @pl.when(core != side)
        def _():
            whole = dst.at[pl.ds(0, n_z * tok)]
            pltpu.make_async_copy(whole, whole, ss.at[i]).wait()

        @pl.when(me == blocks)
        def _():
            whole = dst.at[pl.ds(0, (n_z - 1) * (tok // 2))]
            pltpu.make_async_copy(whole, whole, sso.at[i]).wait()

    pltpu.make_async_copy(outf, outf, s_out.at[0]).wait()
    store.wait()


def solution(mesh):
    n_sec, n_dp = mesh.shape["section"], mesh.shape["dp"]
    n_z = n_dp // 2

    def on_device(acts, output_gradient, gains, down, up, thresholds, lengths, owners):
        tok, feat = acts.shape[2:]
        rank = down.shape[2]
        half = feat // 2
        per_chip = feat // n_z
        win = -(-per_chip // LANE) * LANE
        pieces, blocks = tok // R, n_dp // 2
        span = blocks * tok
        long = span + tok // 2
        cols = tok + tok // 2
        hbm = pl.BlockSpec(memory_space=pl.ANY)
        vmem = pl.BlockSpec(memory_space=pltpu.VMEM)
        dma = pltpu.SemaphoreType.DMA
        packed = pltpu.VMEM((pieces, 2 * R, half), BF16)
        whole = pltpu.VMEM((tok, feat), BF16)
        ig, lora, owned = pl.pallas_call(
            functools.partial(kernel, n_sec, n_dp),
            out_shape=(
                jax.ShapeDtypeStruct((tok, feat), BF16),
                jax.ShapeDtypeStruct((feat // n_dp, 2 * rank), F32),
                jax.ShapeDtypeStruct((1, OWN), F32),
            ),
            in_specs=[hbm, hbm, vmem, hbm, hbm, vmem, vmem, vmem],
            out_specs=(hbm, hbm, vmem),
            scratch_shapes=[
                whole,
                whole,
                pltpu.VMEM((half, 2 * rank), BF16),
                pltpu.VMEM((feat, rank), BF16),
                pltpu.VMEM((2 * rank, half), BF16),
                whole,
                packed,
                packed,
                packed,
                whole,
                pltpu.VMEM((tok, LANE), F32),
                pltpu.VMEM((tok, rank), F32),
                pltpu.VMEM((tok, rank), BF16),
                pltpu.VMEM((tok, rank), F32),
                pltpu.VMEM((tok, rank), BF16),
                pltpu.VMEM((long, win), BF16),
                pltpu.VMEM((long, win), BF16),
                pltpu.VMEM((long, rank), BF16),
                pltpu.VMEM((long, rank), BF16),
                pltpu.VMEM((blocks, tok, cols), F32),
                pltpu.VMEM((blocks, tok, cols), F32),
                pltpu.VMEM((n_dp, 8, LANE), F32),
                pltpu.VMEM((win, 2 * rank), F32),
                pltpu.VMEM((per_chip // 2, 2 * rank), F32),
                pltpu.VMEM((per_chip // 2, 2 * rank), F32),
                pltpu.VMEM((rank, span), F32),
                pltpu.VMEM((rank, span), F32),
                pltpu.VMEM((8, span + tok), F32),
                pltpu.VMEM((span + tok, LANE), F32),
                dma((5,)),
                dma((2,)),
                dma((pieces, CHUNKS)),
                dma,
                dma((4,)),
                dma((4,)),
                dma((4,)),
                dma((4,)),
                dma,
                dma,
                dma,
                dma,
            ],
            compiler_params=pltpu.CompilerParams(
                collective_id=0, has_side_effects=True, vmem_limit_bytes=56 << 20
            ),
        )(acts[0, 0], output_gradient[0], gains, down[0], up[0], thresholds[0], lengths, owners)
        return ig[None, None], lora[None], owned[None]

    placed = (
        P("section", None, "dp", None),
        P(None, "dp", None),
        P("section", None),
        P("section", None, None),
        P("section", None, None),
        P("section", None, None),
        P(),
        P(),
    )
    return jax.shard_map(
        on_device,
        mesh=mesh,
        in_specs=placed,
        out_specs=(P("section", None, "dp", None), P("section", "dp", None), P("section", None, "dp")),
        check_vma=False,
    )
```

```python
import functools

import jax
import jax.numpy as jnp
from jax import lax
from jax.experimental import pallas as pl
from jax.experimental.pallas import tpu as pltpu
from jax.sharding import PartitionSpec as P

OWN = 8
NORM_EPS = 1e-06
MESH = pl.DeviceIdType.MESH
F32, BF16 = jnp.float32, jnp.bfloat16
R = 8
G = 16
LANE = 128
CHUNKS = 3
LATE = 2


def dot(a, b):
    return jnp.dot(a, b, preferred_element_type=F32)


def dot_nt(a, b):
    return lax.dot_general(a, b, (((1,), (1,)), ((), ())), preferred_element_type=F32)


def halves(v, half):
    return jnp.concatenate([v[:, :half], v[:, half:]], axis=0)


def kernel(n_sec, n_dp, *refs):
    (acts, og, gains, dn, up, thr, lens, own, ig, lora, owned,
     xv, flat, ucat, dv, dtc, normed, xp, arr, outp, outf, scale, hidf, hidb, lowf, stage,
     r_n, r_a, r_h, nw, hw, parts, part_f, other, lora_v, hid_t, low_t, doc_row, doc_col,
     s_load, s_out, s_chain, c_send, rs, rso, ss, sso, p_send, p_recv, o_send, o_recv) = refs
    tok, feat = xv.shape
    half = feat // 2
    n_docs = lens.shape[1]
    pieces, groups = tok // R, tok // G
    n_z = n_dp // 2
    per_chip = feat // n_z
    win = r_n.shape[1]
    blocks = n_dp // 2
    span = blocks * tok
    cols = tok + tok // 2
    lanes = half // CHUNKS

    sec = lax.axis_index("section")
    me = lax.axis_index("dp")
    z, core = me // 2, lax.rem(me, 2)
    side = me // blocks
    slot = lax.rem(me, blocks)
    last = n_sec - 1
    first_half = core == 0

    def load(src, dst, i):
        return pltpu.make_async_copy(src, dst, s_load.at[i])

    loads = [
        load(acts, xv, 0),
        load(dn, dv, 1),
        load(up.at[pl.ds(0, half)], ucat.at[:, pl.ds(0, LANE)], 2),
        load(up.at[pl.ds(half, half)], ucat.at[:, pl.ds(LANE, LANE)], 3),
    ]
    for c in loads:
        c.start()

    @pl.when(sec == last)
    def _():
        load(og, flat, 4).start()

    barrier = pltpu.get_barrier_semaphore()

    def greet(who):
        pl.semaphore_signal(barrier, inc=1, device_id=who, device_id_type=MESH)

    @pl.when(sec > 0)
    def _():
        greet({"section": sec - 1})

    @pl.when(sec < last)
    def _():
        greet({"section": sec + 1})

    for peer in range(n_dp):
        @pl.when(me != peer)
        def _():
            greet({"dp": peer})

    @pl.when(core == 1)
    def _():
        for r in (r_n, r_a, r_h):
            r[pl.ds(span, tok // 2), :] = jnp.zeros((tok // 2, r.shape[1]), BF16)

    loads[0].wait()

    def norm_group(q, _):
        rows = pl.ds(pl.multiple_of(q * G, G), G)
        v = xv[rows, :].astype(F32)
        s = lax.rsqrt(jnp.sum(v * v, axis=1, keepdims=True) / feat + NORM_EPS)
        scale[rows, :] = jnp.broadcast_to(s, (G, LANE))
        normed[rows, :] = (v * s * gains[...]).astype(BF16)
        xp[2 * q] = halves(v[:R], half).astype(BF16)
        xp[2 * q + 1] = halves(v[R:], half).astype(BF16)
        return 0

    lax.fori_loop(0, groups, norm_group, 0)
    loads[1].wait()
    hidf[...] = jnp.zeros_like(hidf)

    def down_tile(t, _):
        here = pl.ds(pl.multiple_of(t * LANE, LANE), LANE)
        there = pl.ds(pl.multiple_of(t * LANE + half, LANE), LANE)
        dtc[pl.ds(0, LANE), here] = (dv[here, :].astype(F32).T * gains[:, here]).astype(BF16)
        dtc[pl.ds(LANE, LANE), here] = (dv[there, :].astype(F32).T * gains[:, there]).astype(BF16)
        hidf[...] += dot(normed[:, here], dv[here, :]) + dot(normed[:, there], dv[there, :])
        return 0

    lax.fori_loop(0, half // LANE, down_tile, 0)
    hidb[...] = hidf[...].astype(BF16)

    @pl.when(sec == last)
    def _():
        load(og, flat, 4).wait()

        def pack(q, _):
            rows = pl.ds(pl.multiple_of(q * G, G), G)
            v = flat[rows, :].astype(F32)
            arr[2 * q] = halves(v[:R], half).astype(BF16)
            arr[2 * q + 1] = halves(v[R:], half).astype(BF16)
            return 0

        lax.fori_loop(0, groups, pack, 0)

    loads[2].wait()
    loads[3].wait()

    ends = jnp.where(sec > 0, 1, 0) + jnp.where(sec < last, 1, 0)
    pl.semaphore_wait(barrier, n_dp - 1 + ends)

    def send(src, dst, i, zz, dest_core, row, n, sems):
        at = pl.multiple_of(row, G)
        d = dst.at[pl.ds(at, n), :]
        dest = 2 * zz + dest_core

        @pl.when(dest == me)
        def _():
            pltpu.make_async_copy(src, d, sems[1].at[i]).start()

        @pl.when(dest != me)
        def _():
            pltpu.make_async_remote_copy(
                src_ref=src, dst_ref=d, send_sem=sems[0].at[i], recv_sem=sems[1].at[i],
                device_id={"dp": dest}, device_id_type=MESH,
            ).start()

    def spread_own(zz):
        start = pl.multiple_of(per_chip * zz // LANE * LANE, LANE)
        there = pl.ds(start, win)
        send(normed.at[:, there], r_n, 0, zz, side, slot * tok, tok, (ss, rs))
        send(hidb, r_h, 1, zz, side, slot * tok, tok, (ss, rs))

        @pl.when(me == blocks)
        def _():
            top = pl.ds(0, tok // 2)
            send(normed.at[top, there], r_n, 0, zz, 0, span, tok // 2, (sso, rso))
            send(hidb.at[top], r_h, 1, zz, 0, span, tok // 2, (sso, rso))

    def spread_all(zz, _):
        spread_own(zz)
        return 0

    def spread_arriving(q):
        row = q * G
        a, b = arr[2 * q].astype(F32), arr[2 * q + 1].astype(F32)
        low = lowf[pl.ds(pl.multiple_of(row, G), G), :].astype(BF16)
        lane = lax.broadcasted_iota(jnp.int32, (1, LANE), 1)
        for zz in range(n_z):
            first = per_chip * zz
            start = first // LANE * LANE
            part = start // half
            r0, l0 = part * R, start - part * half
            w = jnp.concatenate([a[r0:r0 + R, l0:l0 + win], b[r0:r0 + R, l0:l0 + win]], axis=0)
            w = jnp.concatenate([
                w[:, :LANE] * jnp.where(lane >= first - start, 1.0, 0.0),
                w[:, LANE:win - LANE],
                w[:, win - LANE:] * jnp.where(lane < first + per_chip - (start + win - LANE), 1.0, 0.0),
            ], axis=1)
            stage[q, zz, :, pl.ds(0, win)] = w.astype(BF16)
            stage[q, zz, :, pl.ds(win, LANE)] = low
        for zz in range(n_z):
            send(stage.at[q, zz], r_a, 2, zz, side, slot * tok + row, G, (ss, rs))

            @pl.when((me == blocks) & (row < tok // 2))
            def _():
                send(stage.at[q, zz], r_a, 2, zz, 0, span + lax.rem(row, tok // 2), G, (sso, rso))

    def doc_tables():
        k_row = lax.broadcasted_iota(jnp.int32, (n_docs, n_docs), 1)
        k_col = lax.broadcasted_iota(jnp.int32, (n_docs, n_docs), 0)
        len_row = lens[...].astype(F32)
        len_col = jnp.sum(jnp.where(k_row == k_col, len_row, 0.0), axis=1, keepdims=True)
        ends_col = jnp.sum(jnp.where(k_row <= k_col, len_row, 0.0), axis=1, keepdims=True)
        ends_row = jnp.sum(jnp.where(k_col <= k_row, len_col, 0.0), axis=0, keepdims=True)
        base = core * span

        def at(b, _):
            start = pl.multiple_of(b * tok, tok)
            pos_r = (lax.broadcasted_iota(jnp.int32, (n_docs, tok), 1) + (base + start)).astype(F32)
            doc_row[:, pl.ds(start, tok)] = jnp.broadcast_to(
                jnp.sum(jnp.where(ends_col <= pos_r, 1.0, 0.0), axis=0, keepdims=True), (8, tok))
            pos_c = (lax.broadcasted_iota(jnp.int32, (tok, n_docs), 0) + (base + start)).astype(F32)
            doc_col[pl.ds(start, tok), :] = jnp.broadcast_to(
                jnp.sum(jnp.where(ends_row <= pos_c, 1.0, 0.0), axis=1, keepdims=True), (tok, LANE))
            return 0

        lax.fori_loop(0, blocks + 1, at, 0)

    early = sec < n_sec - LATE

    @pl.when(early)
    def _():
        lax.fori_loop(0, n_z, spread_all, 0)

    def chain_copy(p, c):
        there = pl.ds(c * lanes, lanes)
        return pltpu.make_async_remote_copy(
            src_ref=outp.at[p, :, there], dst_ref=arr.at[p, :, there],
            send_sem=c_send, recv_sem=s_chain.at[p, c],
            device_id={"section": jnp.maximum(sec - 1, 0)}, device_id_type=MESH,
        )

    def piece(p):
        row = pl.multiple_of(p * R, R)
        rows = pl.ds(row, R)
        both = jnp.zeros((2 * R, 2 * LANE), F32)
        for c in range(CHUNKS):
            @pl.when(sec < last)
            def _():
                chain_copy(p, c).wait_recv()

            there = pl.ds(c * lanes, lanes)
            both += dot(arr[p, :, there], ucat[there, :])
        low = (both[:R, :LANE] + both[R:, LANE:]).astype(BF16).astype(F32)
        lowf[rows, :] = low
        s = scale[rows, :1]
        k = s * s * (jnp.sum(low * hidf[rows, :], axis=1, keepdims=True) / feat)
        zero = jnp.zeros_like(low)
        wide = jnp.concatenate(
            [jnp.concatenate([low, zero], axis=1), jnp.concatenate([zero, low], axis=1)], axis=0
        ).astype(BF16)
        s2, k2 = jnp.concatenate([s, s], axis=0), jnp.concatenate([k, k], axis=0)
        for c in range(CHUNKS):
            there = pl.ds(c * lanes, lanes)
            back = dot(wide, dtc[:, there])
            out = arr[p, :, there].astype(F32) + s2 * back - k2 * xp[p, :, there].astype(F32)
            outp[p, :, there] = out.astype(BF16)

            @pl.when(sec > 0)
            def _():
                chain_copy(p, c).start()

    def group(q, _):
        piece(2 * q)
        piece(2 * q + 1)
        row = pl.multiple_of(q * G, G)
        rows = pl.ds(row, G)

        def unpack(src):
            a, b = src[2 * q].astype(F32), src[2 * q + 1].astype(F32)
            return (jnp.concatenate([a[:R], b[:R]], axis=0).astype(BF16),
                    jnp.concatenate([a[R:], b[R:]], axis=0).astype(BF16))

        lo, hi = unpack(outp)
        outf[rows, pl.ds(0, half)] = lo
        outf[rows, pl.ds(half, half)] = hi
        spread_arriving(q)

        @pl.when(jnp.logical_not(early))
        def _():
            spread_own(q)

        pltpu.make_async_copy(outf.at[rows], ig.at[rows], s_out.at[0]).start()
        return 0

    lax.fori_loop(0, groups, group, 0)

    def arrived(dst, i):
        pltpu.make_async_copy(dst.at[pl.ds(0, span)], dst.at[pl.ds(0, span)], rs.at[i]).wait()

        @pl.when(first_half)
        def _():
            over = dst.at[pl.ds(span, tok // 2)]
            pltpu.make_async_copy(over, over, rso.at[i]).wait()

    doc_tables()
    arrived(r_n, 0)
    arrived(r_h, 1)
    offset = lax.rem(z, 2) * (LANE // 2)
    lane = lax.broadcasted_iota(jnp.int32, (1, win), 1)
    inside = jnp.where((lane >= offset) & (lane < offset + per_chip), 1.0, 0.0)
    column = jnp.where(lax.broadcasted_iota(jnp.int32, (1, cols), 1) < tok, 1.0, 2.0)

    def mine(src, b):
        return (src[pl.ds(b * tok, tok), :].astype(F32) * inside).astype(BF16)

    for b in range(blocks):
        there = pl.ds(b * tok, cols)
        same = doc_col[pl.ds(b * tok, tok), :1] == doc_row[:1, there]
        weight = jnp.where(same, column, 0.0)
        nw[b] = weight * dot_nt(mine(r_n, b), r_n[there, :])
        hw[b] = weight * dot_nt(r_h[pl.ds(b * tok, tok), :], r_h[there, :])
        hid_t[:, pl.ds(b * tok, tok)] = r_h[pl.ds(b * tok, tok), :].astype(F32).T

    arrived(r_a, 2)
    win_l, low_l = pl.ds(0, win), pl.ds(win, LANE)
    total = jnp.zeros((1, LANE), F32)
    doc_lane = lax.broadcasted_iota(jnp.int32, (tok, LANE), 1).astype(F32)
    for b in range(blocks):
        there, here = pl.ds(b * tok, cols), pl.ds(b * tok, tok)
        pair = nw[b] * dot_nt(r_a[here, low_l], r_a[there, low_l]) + hw[b] * dot_nt(r_a[here, win_l], r_a[there, win_l])
        row_sum = jnp.sum(pair, axis=1, keepdims=True)
        total += jnp.sum(jnp.where(doc_col[here, :] == doc_lane, row_sum, 0.0), axis=0, keepdims=True)
    parts[me] = jnp.broadcast_to(total, (8, LANE))

    for peer in range(n_dp):
        @pl.when(me != peer)
        def _():
            pltpu.make_async_remote_copy(
                src_ref=parts.at[me], dst_ref=parts.at[me], send_sem=p_send, recv_sem=p_recv,
                device_id={"dp": peer}, device_id_type=MESH,
            ).start()

    for b in range(blocks):
        here = pl.ds(b * tok, tok)
        low_t[:, here] = r_a[here, low_l].astype(F32).T

    most = parts.at[pl.ds(0, n_dp - 1)]
    pltpu.make_async_copy(most, most, p_recv).wait()
    pair_sum = jnp.sum(parts[...], axis=0)[:1, :n_docs]
    ratio = jnp.sqrt(pair_sum / (feat * LANE) + NORM_EPS) / thr[...]
    clip = jnp.minimum(1.0, 1.0 / ratio)
    k_row = lax.broadcasted_iota(jnp.int32, (n_docs, n_docs), 1)
    k_col = lax.broadcasted_iota(jnp.int32, (n_docs, n_docs), 0)
    clip_col = jnp.sum(jnp.where(k_row == k_col, clip, 0.0), axis=1, keepdims=True)
    doc_id = lax.broadcasted_iota(jnp.int32, (n_docs, span), 0).astype(F32)
    token_clip = jnp.sum(
        jnp.where(doc_row[:1, pl.ds(0, span)] == doc_id, clip_col, 0.0), axis=0, keepdims=True)
    down = dot((low_t[...] * token_clip).astype(BF16), r_n[pl.ds(0, span), :])
    up_g = dot((hid_t[...] * token_clip).astype(BF16), r_a[pl.ds(0, span), win_l])
    part_f[:, pl.ds(0, LANE)] = down.T
    part_f[:, pl.ds(LANE, LANE)] = up_g.T
    own_rows = pl.multiple_of(offset + core * (per_chip // 2), 8)
    far_rows = pl.multiple_of(offset + (1 - core) * (per_chip // 2), 8)
    swap = pltpu.make_async_remote_copy(
        src_ref=part_f.at[pl.ds(far_rows, per_chip // 2)], dst_ref=other,
        send_sem=o_send, recv_sem=o_recv,
        device_id={"dp": 2 * z + (1 - core)}, device_id_type=MESH,
    )
    swap.start()

    own_row = jnp.where(own[...] == me, 1.0, 0.0)
    own_col = jnp.sum(jnp.where(k_row == k_col, own_row, 0.0), axis=1, keepdims=True)
    rank_col = jnp.sum(jnp.where(k_row <= k_col, own_row, 0.0), axis=1, keepdims=True) - 1.0
    ratio_col = jnp.sum(jnp.where(k_row == k_col, ratio, 0.0), axis=1, keepdims=True)
    slot_id = lax.broadcasted_iota(jnp.int32, (n_docs, OWN), 1).astype(F32)
    held = jnp.where((own_col > 0.5) & (rank_col == slot_id), ratio_col, 0.0)
    owned[...] = jnp.sum(held, axis=0, keepdims=True)

    swap.wait()
    lora_v[...] = (part_f[pl.ds(own_rows, per_chip // 2), :] + other[...]) / n_docs
    store = pltpu.make_async_copy(lora_v, lora, s_out.at[1])
    store.start()

    pltpu.make_async_copy(most, most, p_send).wait()

    @pl.when(sec > 0)
    def _():
        pltpu.make_async_copy(outp, outp, c_send).wait()

    for i, dst in enumerate((r_n, r_h, r_a)):
        @pl.when(core == side)
        def _():
            whole = dst.at[pl.ds(0, (n_z - 1) * tok)]
            pltpu.make_async_copy(whole, whole, ss.at[i]).wait()

        @pl.when(core != side)
        def _():
            whole = dst.at[pl.ds(0, n_z * tok)]
            pltpu.make_async_copy(whole, whole, ss.at[i]).wait()

        @pl.when(me == blocks)
        def _():
            whole = dst.at[pl.ds(0, (n_z - 1) * (tok // 2))]
            pltpu.make_async_copy(whole, whole, sso.at[i]).wait()

    pltpu.make_async_copy(outf, outf, s_out.at[0]).wait()
    store.wait()


def solution(mesh):
    n_sec, n_dp = mesh.shape["section"], mesh.shape["dp"]
    n_z = n_dp // 2

    def on_device(acts, output_gradient, gains, down, up, thresholds, lengths, owners):
        tok, feat = acts.shape[2:]
        rank = down.shape[2]
        half = feat // 2
        per_chip = feat // n_z
        win = -(-per_chip // LANE) * LANE
        pieces, blocks = tok // R, n_dp // 2
        span = blocks * tok
        long = span + tok // 2
        cols = tok + tok // 2
        hbm = pl.BlockSpec(memory_space=pl.ANY)
        vmem = pl.BlockSpec(memory_space=pltpu.VMEM)
        dma = pltpu.SemaphoreType.DMA
        packed = pltpu.VMEM((pieces, 2 * R, half), BF16)
        whole = pltpu.VMEM((tok, feat), BF16)
        ig, lora, owned = pl.pallas_call(
            functools.partial(kernel, n_sec, n_dp),
            out_shape=(
                jax.ShapeDtypeStruct((tok, feat), BF16),
                jax.ShapeDtypeStruct((feat // n_dp, 2 * rank), F32),
                jax.ShapeDtypeStruct((1, OWN), F32),
            ),
            in_specs=[hbm, hbm, vmem, hbm, hbm, vmem, vmem, vmem],
            out_specs=(hbm, hbm, vmem),
            scratch_shapes=[
                whole,
                whole,
                pltpu.VMEM((half, 2 * rank), BF16),
                pltpu.VMEM((feat, rank), BF16),
                pltpu.VMEM((2 * rank, half), BF16),
                whole,
                packed,
                packed,
                packed,
                whole,
                pltpu.VMEM((tok, LANE), F32),
                pltpu.VMEM((tok, rank), F32),
                pltpu.VMEM((tok, rank), BF16),
                pltpu.VMEM((tok, rank), F32),
                pltpu.VMEM((tok // G, n_z, G, win + rank), BF16),
                pltpu.VMEM((long, win), BF16),
                pltpu.VMEM((long, win + rank), BF16),
                pltpu.VMEM((long, rank), BF16),
                pltpu.VMEM((blocks, tok, cols), F32),
                pltpu.VMEM((blocks, tok, cols), F32),
                pltpu.VMEM((n_dp, 8, LANE), F32),
                pltpu.VMEM((win, 2 * rank), F32),
                pltpu.VMEM((per_chip // 2, 2 * rank), F32),
                pltpu.VMEM((per_chip // 2, 2 * rank), F32),
                pltpu.VMEM((rank, span), F32),
                pltpu.VMEM((rank, span), F32),
                pltpu.VMEM((8, span + tok), F32),
                pltpu.VMEM((span + tok, LANE), F32),
                dma((5,)),
                dma((2,)),
                dma((pieces, CHUNKS)),
                dma,
                dma((3,)),
                dma((3,)),
                dma((3,)),
                dma((3,)),
                dma,
                dma,
                dma,
                dma,
            ],
            compiler_params=pltpu.CompilerParams(
                collective_id=0, has_side_effects=True, vmem_limit_bytes=56 << 20
            ),
        )(acts[0, 0], output_gradient[0], gains, down[0], up[0], thresholds[0], lengths, owners)
        return ig[None, None], lora[None], owned[None]

    placed = (
        P("section", None, "dp", None),
        P(None, "dp", None),
        P("section", None),
        P("section", None, None),
        P("section", None, None),
        P("section", None, None),
        P(),
        P(),
    )
    return jax.shard_map(
        on_device,
        mesh=mesh,
        in_specs=placed,
        out_specs=(P("section", None, "dp", None), P("section", "dp", None), P("section", None, "dp")),
        check_vma=False,
    )
```

```python
import functools

import jax
import jax.numpy as jnp
from jax import lax
from jax.experimental import pallas as pl
from jax.experimental.pallas import tpu as pltpu
from jax.sharding import PartitionSpec as P

OWN = 8
NORM_EPS = 1e-06
MESH = pl.DeviceIdType.MESH
F32, BF16 = jnp.float32, jnp.bfloat16
R = 4
Q = 4
L = 8
G = 16
LANE = 128
CHUNKS = 3
LATE = 2


def dot(a, b):
    return jnp.dot(a, b, preferred_element_type=F32)


def dot_nt(a, b):
    return lax.dot_general(a, b, (((1,), (1,)), ((), ())), preferred_element_type=F32)


def pick(top, bottom):
    row = lax.broadcasted_iota(jnp.int32, top.shape, 0)
    return jnp.where(row < R, top, bottom)


def turn(v):
    return pltpu.roll(v, R, 0)


def pack(v, width):
    a, b, c, d = [v[:, q * width:(q + 1) * width] for q in range(Q)]
    first = jnp.concatenate([pick(a, turn(b)), pick(c, turn(d))], axis=0)
    second = jnp.concatenate([pick(turn(a), b), pick(turn(c), d)], axis=0)
    return first.astype(BF16), second.astype(BF16)


def unpack(first, second):
    first, second = first.astype(F32), second.astype(F32)
    out = []
    for h in range(Q // 2):
        a, b = first[h * L:(h + 1) * L], second[h * L:(h + 1) * L]
        out += [pick(a, turn(b)), pick(turn(a), b)]
    return out


def doubled(v):
    w = turn(v)
    return pick(v, w), pick(w, v)


def fold(both):
    t = [both[(q // 2) * L:(q // 2 + 1) * L, q * LANE:(q + 1) * LANE] for q in range(Q)]
    y = pick(t[0], t[1]) + pick(t[2], t[3])
    return y + turn(y)


def widen(low):
    zero = jnp.zeros_like(low)
    upper, lower = pick(low, zero), pick(zero, low)
    return jnp.concatenate([
        jnp.concatenate([upper, lower, zero, zero], axis=1),
        jnp.concatenate([zero, zero, upper, lower], axis=1),
    ], axis=0).astype(BF16)


def kernel(n_sec, n_dp, *refs):
    (acts, og, gains, dn, up, thr, lens, own, ig, lora, owned,
     xv, flat, ucat, dv, dtc, normed, xp, arr, outp, scale, hidf, hidb, hidp, lowp, stage,
     r_n, r_a, r_h, nw, hw, parts, part_f, other, hid_t, low_t, doc_row, doc_col,
     s_load, s_chain, c_send, rs, rso, ss, sso, p_send, p_recv, o_send, o_recv) = refs
    tok, feat = xv.shape
    width = feat // Q
    n_docs = lens.shape[1]
    pieces, groups = tok // R, tok // G
    n_z = n_dp // 2
    per_chip = feat // n_z
    win = r_n.shape[1]
    blocks = n_dp // 2
    span = blocks * tok
    cols = tok + tok // 2
    lanes = width // CHUNKS

    sec = lax.axis_index("section")
    me = lax.axis_index("dp")
    z, core = me // 2, lax.rem(me, 2)
    side = me // blocks
    slot = lax.rem(me, blocks)
    last = n_sec - 1
    first_half = core == 0

    def load(src, dst, i):
        return pltpu.make_async_copy(src, dst, s_load.at[i])

    loads = [load(dn, dv, 0), load(acts, xv, 1)] + [
        load(up.at[pl.ds(q * width, width)], ucat.at[:, pl.ds(q * LANE, LANE)], 2 + q) for q in range(Q)
    ]
    for c in loads:
        c.start()

    @pl.when(sec == last)
    def _():
        load(og, flat, 2 + Q).start()

    barrier = pltpu.get_barrier_semaphore()

    def greet(who):
        pl.semaphore_signal(barrier, inc=1, device_id=who, device_id_type=MESH)

    @pl.when(sec > 0)
    def _():
        greet({"section": sec - 1})

    @pl.when(sec < last)
    def _():
        greet({"section": sec + 1})

    for peer in range(n_dp):
        @pl.when(me != peer)
        def _():
            greet({"dp": peer})

    @pl.when(core == 1)
    def _():
        for r in (r_n, r_a, r_h):
            r[pl.ds(span, tok // 2), :] = jnp.zeros((tok // 2, r.shape[1]), BF16)

    loads[0].wait()

    def turn_map(t, _):
        here = pl.ds(pl.multiple_of(t * LANE, LANE), LANE)
        for q in range(Q):
            there = pl.ds(pl.multiple_of(t * LANE + q * width, LANE), LANE)
            dtc[pl.ds(q * LANE, LANE), here] = (dv[there, :].astype(F32).T * gains[:, there]).astype(BF16)
        return 0

    lax.fori_loop(0, width // LANE, turn_map, 0)
    loads[1].wait()

    def norm_group(q, _):
        rows = pl.ds(pl.multiple_of(q * G, G), G)
        v = xv[rows, :].astype(F32)
        s = lax.rsqrt(jnp.sum(v * v, axis=1, keepdims=True) / feat + NORM_EPS)
        normed[rows, :] = (v * s * gains[...]).astype(BF16)
        for h in range(G // L):
            p = q * (G // R) + 2 * h
            own_rows = slice(h * L, (h + 1) * L)
            xp[p], xp[p + 1] = pack(v[own_rows], width)
            scale[p], scale[p + 1] = doubled(jnp.broadcast_to(s[own_rows], (L, LANE)))
        return 0

    lax.fori_loop(0, groups, norm_group, 0)
    hidf[...] = jnp.zeros_like(hidf)

    def down_part(t, _):
        here = pl.ds(pl.multiple_of(t * (width // 3), LANE), width // 3)
        hidf[...] += dot(normed[:, here], dv[here, :])
        return 0

    lax.fori_loop(0, 3 * Q, down_part, 0)
    hidb[...] = hidf[...].astype(BF16)
    for h in range(tok // L):
        hidp[2 * h], hidp[2 * h + 1] = doubled(hidf[pl.ds(h * L, L), :])

    @pl.when(sec == last)
    def _():
        load(og, flat, 2 + Q).wait()

        def pack_group(q, _):
            rows = pl.ds(pl.multiple_of(q * G, G), G)
            v = flat[rows, :].astype(F32)
            for h in range(G // L):
                p = q * (G // R) + 2 * h
                arr[p], arr[p + 1] = pack(v[h * L:(h + 1) * L], width)
            return 0

        lax.fori_loop(0, groups, pack_group, 0)

    for c in loads[2:]:
        c.wait()
    ends = jnp.where(sec > 0, 1, 0) + jnp.where(sec < last, 1, 0)
    pl.semaphore_wait(barrier, n_dp - 1 + ends)

    def send(src, dst, i, zz, dest_core, row, n, sems):
        at = pl.multiple_of(row, G)
        d = dst.at[pl.ds(at, n), :]
        dest = 2 * zz + dest_core

        @pl.when(dest == me)
        def _():
            pltpu.make_async_copy(src, d, sems[1].at[i]).start()

        @pl.when(dest != me)
        def _():
            pltpu.make_async_remote_copy(
                src_ref=src, dst_ref=d, send_sem=sems[0].at[i], recv_sem=sems[1].at[i],
                device_id={"dp": dest}, device_id_type=MESH,
            ).start()

    def spread_own(zz):
        start = pl.multiple_of(per_chip * zz // LANE * LANE, LANE)
        there = pl.ds(start, win)
        send(normed.at[:, there], r_n, 0, zz, side, slot * tok, tok, (ss, rs))
        send(hidb, r_h, 1, zz, side, slot * tok, tok, (ss, rs))

        @pl.when(me == blocks)
        def _():
            top = pl.ds(0, tok // 2)
            send(normed.at[top, there], r_n, 0, zz, 0, span, tok // 2, (sso, rso))
            send(hidb.at[top], r_h, 1, zz, 0, span, tok // 2, (sso, rso))

    def spread_all(zz, _):
        spread_own(zz)
        return 0

    def whole_rows(src, q):
        p = q * (G // R)
        both = [unpack(src[p + 2 * h], src[p + 2 * h + 1]) for h in range(G // L)]
        return [jnp.concatenate(x, axis=0) for x in zip(*both)]

    def spread_arriving(q):
        row = q * G
        quarters = whole_rows(arr, q)
        p = q * (G // R)
        low = jnp.concatenate(
            [pick(lowp[p + 2 * h], lowp[p + 2 * h + 1]) for h in range(G // L)], axis=0).astype(BF16)
        lane = lax.broadcasted_iota(jnp.int32, (1, LANE), 1)
        for zz in range(n_z):
            first = per_chip * zz
            start = first // LANE * LANE
            part = start // width
            l0 = start - part * width
            w = quarters[part][:, l0:l0 + win]
            w = jnp.concatenate([
                w[:, :LANE] * jnp.where(lane >= first - start, 1.0, 0.0),
                w[:, LANE:win - LANE],
                w[:, win - LANE:] * jnp.where(lane < first + per_chip - (start + win - LANE), 1.0, 0.0),
            ], axis=1)
            stage[q, zz, :, pl.ds(0, win)] = w.astype(BF16)
            stage[q, zz, :, pl.ds(win, LANE)] = low
        for zz in range(n_z):
            send(stage.at[q, zz], r_a, 2, zz, side, slot * tok + row, G, (ss, rs))

            @pl.when((me == blocks) & (row < tok // 2))
            def _():
                send(stage.at[q, zz], r_a, 2, zz, 0, span + lax.rem(row, tok // 2), G, (sso, rso))

    def doc_tables():
        k_row = lax.broadcasted_iota(jnp.int32, (n_docs, n_docs), 1)
        k_col = lax.broadcasted_iota(jnp.int32, (n_docs, n_docs), 0)
        len_row = lens[...].astype(F32)
        len_col = jnp.sum(jnp.where(k_row == k_col, len_row, 0.0), axis=1, keepdims=True)
        ends_col = jnp.sum(jnp.where(k_row <= k_col, len_row, 0.0), axis=1, keepdims=True)
        ends_row = jnp.sum(jnp.where(k_col <= k_row, len_col, 0.0), axis=0, keepdims=True)
        base = core * span

        def at(b, _):
            start = pl.multiple_of(b * tok, tok)
            pos_r = (lax.broadcasted_iota(jnp.int32, (n_docs, tok), 1) + (base + start)).astype(F32)
            doc_row[:, pl.ds(start, tok)] = jnp.broadcast_to(
                jnp.sum(jnp.where(ends_col <= pos_r, 1.0, 0.0), axis=0, keepdims=True), (8, tok))
            pos_c = (lax.broadcasted_iota(jnp.int32, (tok, n_docs), 0) + (base + start)).astype(F32)
            doc_col[pl.ds(start, tok), :] = jnp.broadcast_to(
                jnp.sum(jnp.where(ends_row <= pos_c, 1.0, 0.0), axis=1, keepdims=True), (tok, LANE))
            return 0

        lax.fori_loop(0, blocks + 1, at, 0)

    early = sec < n_sec - LATE

    @pl.when(early)
    def _():
        lax.fori_loop(0, n_z, spread_all, 0)

    def chain_copy(p, c):
        there = pl.ds(c * lanes, lanes)
        return pltpu.make_async_remote_copy(
            src_ref=outp.at[p, :, there], dst_ref=arr.at[p, :, there],
            send_sem=c_send, recv_sem=s_chain.at[p, c],
            device_id={"section": jnp.maximum(sec - 1, 0)}, device_id_type=MESH,
        )

    parts_of = [pl.ds(c * lanes, lanes) for c in range(CHUNKS)]

    def piece(p, recv, send_on):
        both = jnp.zeros((2 * L, Q * LANE), F32)
        for c, there in enumerate(parts_of):
            if recv:
                chain_copy(p, c).wait_recv()
            both += dot(arr[p, :, there], ucat[there, :])
        low = fold(both).astype(BF16).astype(F32)
        s = scale[p][:, :1]
        k = s * s * (jnp.sum(low * hidp[p], axis=1, keepdims=True) / feat)
        s2, k2 = jnp.concatenate([s, s], axis=0), jnp.concatenate([k, k], axis=0)
        wide = widen(low)
        for c, there in enumerate(parts_of):
            out = arr[p, :, there].astype(F32) + s2 * dot(wide, dtc[:, there]) - k2 * xp[p, :, there].astype(F32)
            outp[p, :, there] = out.astype(BF16)
            if send_on:
                chain_copy(p, c).start()
        lowp[p] = low

    def group(q, kind):
        for t in range(G // R):
            piece(q * (G // R) + t, *kind)
        spread_arriving(q)

        @pl.when(jnp.logical_not(early))
        def _():
            spread_own(q)

        rows = pl.ds(pl.multiple_of(q * G, G), G)
        for part, v in enumerate(whole_rows(outp, q)):
            ig[rows, pl.ds(part * width, width)] = v.astype(BF16)

    def run(where, *kind):
        @pl.when(where)
        def _():
            def step(q, _):
                group(q, kind)
                return 0

            lax.fori_loop(0, groups, step, 0)

    run(sec == last, False, True)
    run((sec > 0) & (sec < last), True, True)
    run(sec == 0, True, False)

    def arrived(dst, i):
        pltpu.make_async_copy(dst.at[pl.ds(0, span)], dst.at[pl.ds(0, span)], rs.at[i]).wait()

        @pl.when(first_half)
        def _():
            over = dst.at[pl.ds(span, tok // 2)]
            pltpu.make_async_copy(over, over, rso.at[i]).wait()

    doc_tables()
    arrived(r_n, 0)
    arrived(r_h, 1)
    offset = lax.rem(z, 2) * (LANE // 2)
    lane = lax.broadcasted_iota(jnp.int32, (1, win), 1)
    inside = jnp.where((lane >= offset) & (lane < offset + per_chip), 1.0, 0.0)
    column = jnp.where(lax.broadcasted_iota(jnp.int32, (1, cols), 1) < tok, 1.0, 2.0)

    def mine(src, b):
        return (src[pl.ds(b * tok, tok), :].astype(F32) * inside).astype(BF16)

    for b in range(blocks):
        there = pl.ds(b * tok, cols)
        same = doc_col[pl.ds(b * tok, tok), :1] == doc_row[:1, there]
        weight = jnp.where(same, column, 0.0)
        nw[b] = weight * dot_nt(mine(r_n, b), r_n[there, :])
        hw[b] = weight * dot_nt(r_h[pl.ds(b * tok, tok), :], r_h[there, :])
        hid_t[:, pl.ds(b * tok, tok)] = r_h[pl.ds(b * tok, tok), :].astype(F32).T

    arrived(r_a, 2)
    win_l, low_l = pl.ds(0, win), pl.ds(win, LANE)
    total = jnp.zeros((1, LANE), F32)
    doc_lane = lax.broadcasted_iota(jnp.int32, (tok, LANE), 1).astype(F32)
    for b in range(blocks):
        there, here = pl.ds(b * tok, cols), pl.ds(b * tok, tok)
        pair = nw[b] * dot_nt(r_a[here, low_l], r_a[there, low_l]) + hw[b] * dot_nt(r_a[here, win_l], r_a[there, win_l])
        row_sum = jnp.sum(pair, axis=1, keepdims=True)
        total += jnp.sum(jnp.where(doc_col[here, :] == doc_lane, row_sum, 0.0), axis=0, keepdims=True)
    parts[me] = jnp.broadcast_to(total, (8, LANE))

    for peer in range(n_dp):
        @pl.when(me != peer)
        def _():
            pltpu.make_async_remote_copy(
                src_ref=parts.at[me], dst_ref=parts.at[me], send_sem=p_send, recv_sem=p_recv,
                device_id={"dp": peer}, device_id_type=MESH,
            ).start()

    for b in range(blocks):
        here = pl.ds(b * tok, tok)
        low_t[:, here] = r_a[here, low_l].astype(F32).T

    most = parts.at[pl.ds(0, n_dp - 1)]
    pltpu.make_async_copy(most, most, p_recv).wait()
    pair_sum = jnp.sum(parts[...], axis=0)[:1, :n_docs]
    ratio = jnp.sqrt(pair_sum / (feat * LANE) + NORM_EPS) / thr[...]
    clip = jnp.minimum(1.0, 1.0 / ratio)
    k_row = lax.broadcasted_iota(jnp.int32, (n_docs, n_docs), 1)
    k_col = lax.broadcasted_iota(jnp.int32, (n_docs, n_docs), 0)
    clip_col = jnp.sum(jnp.where(k_row == k_col, clip, 0.0), axis=1, keepdims=True)
    doc_id = lax.broadcasted_iota(jnp.int32, (n_docs, span), 0).astype(F32)
    token_clip = jnp.sum(
        jnp.where(doc_row[:1, pl.ds(0, span)] == doc_id, clip_col, 0.0), axis=0, keepdims=True)
    down = dot((low_t[...] * token_clip).astype(BF16), r_n[pl.ds(0, span), :])
    up_g = dot((hid_t[...] * token_clip).astype(BF16), r_a[pl.ds(0, span), win_l])
    part_f[:, pl.ds(0, LANE)] = down.T
    part_f[:, pl.ds(LANE, LANE)] = up_g.T
    own_rows = pl.multiple_of(offset + core * (per_chip // 2), 8)
    far_rows = pl.multiple_of(offset + (1 - core) * (per_chip // 2), 8)
    swap = pltpu.make_async_remote_copy(
        src_ref=part_f.at[pl.ds(far_rows, per_chip // 2)], dst_ref=other,
        send_sem=o_send, recv_sem=o_recv,
        device_id={"dp": 2 * z + (1 - core)}, device_id_type=MESH,
    )
    swap.start()

    own_row = jnp.where(own[...] == me, 1.0, 0.0)
    own_col = jnp.sum(jnp.where(k_row == k_col, own_row, 0.0), axis=1, keepdims=True)
    rank_col = jnp.sum(jnp.where(k_row <= k_col, own_row, 0.0), axis=1, keepdims=True) - 1.0
    ratio_col = jnp.sum(jnp.where(k_row == k_col, ratio, 0.0), axis=1, keepdims=True)
    slot_id = lax.broadcasted_iota(jnp.int32, (n_docs, OWN), 1).astype(F32)
    held = jnp.where((own_col > 0.5) & (rank_col == slot_id), ratio_col, 0.0)
    owned[...] = jnp.sum(held, axis=0, keepdims=True)

    swap.wait()
    lora[...] = (part_f[pl.ds(own_rows, per_chip // 2), :] + other[...]) / n_docs

    pltpu.make_async_copy(most, most, p_send).wait()

    @pl.when(sec > 0)
    def _():
        pltpu.make_async_copy(outp, outp, c_send).wait()

    for i, dst in enumerate((r_n, r_h, r_a)):
        @pl.when(core == side)
        def _():
            whole = dst.at[pl.ds(0, (n_z - 1) * tok)]
            pltpu.make_async_copy(whole, whole, ss.at[i]).wait()

        @pl.when(core != side)
        def _():
            whole = dst.at[pl.ds(0, n_z * tok)]
            pltpu.make_async_copy(whole, whole, ss.at[i]).wait()

        @pl.when(me == blocks)
        def _():
            whole = dst.at[pl.ds(0, (n_z - 1) * (tok // 2))]
            pltpu.make_async_copy(whole, whole, sso.at[i]).wait()


def solution(mesh):
    n_sec, n_dp = mesh.shape["section"], mesh.shape["dp"]
    n_z = n_dp // 2

    def on_device(acts, output_gradient, gains, down, up, thresholds, lengths, owners):
        tok, feat = acts.shape[2:]
        rank = down.shape[2]
        width = feat // Q
        per_chip = feat // n_z
        win = -(-per_chip // LANE) * LANE
        pieces, blocks = tok // R, n_dp // 2
        span = blocks * tok
        long = span + tok // 2
        cols = tok + tok // 2
        hbm = pl.BlockSpec(memory_space=pl.ANY)
        vmem = pl.BlockSpec(memory_space=pltpu.VMEM)
        dma = pltpu.SemaphoreType.DMA
        packed = pltpu.VMEM((pieces, Q * R, width), BF16)
        whole = pltpu.VMEM((tok, feat), BF16)
        ig, lora, owned = pl.pallas_call(
            functools.partial(kernel, n_sec, n_dp),
            out_shape=(
                pltpu.VMEM((tok, feat), BF16),
                pltpu.VMEM((feat // n_dp, 2 * rank), F32),
                pltpu.VMEM((1, OWN), F32),
            ),
            in_specs=[hbm, hbm, vmem, hbm, hbm, vmem, vmem, vmem],
            out_specs=(vmem, vmem, vmem),
            scratch_shapes=[
                whole,
                whole,
                pltpu.VMEM((width, Q * rank), BF16),
                pltpu.VMEM((feat, rank), BF16),
                pltpu.VMEM((Q * rank, width), BF16),
                whole,
                packed,
                packed,
                packed,
                pltpu.VMEM((pieces, L, LANE), F32),
                pltpu.VMEM((tok, rank), F32),
                pltpu.VMEM((tok, rank), BF16),
                pltpu.VMEM((pieces, L, rank), F32),
                pltpu.VMEM((pieces, L, rank), F32),
                pltpu.VMEM((tok // G, n_z, G, win + rank), BF16),
                pltpu.VMEM((long, win), BF16),
                pltpu.VMEM((long, win + rank), BF16),
                pltpu.VMEM((long, rank), BF16),
                pltpu.VMEM((blocks, tok, cols), F32),
                pltpu.VMEM((blocks, tok, cols), F32),
                pltpu.VMEM((n_dp, 8, LANE), F32),
                pltpu.VMEM((win, 2 * rank), F32),
                pltpu.VMEM((per_chip // 2, 2 * rank), F32),
                pltpu.VMEM((rank, span), F32),
                pltpu.VMEM((rank, span), F32),
                pltpu.VMEM((8, span + tok), F32),
                pltpu.VMEM((span + tok, LANE), F32),
                dma((3 + Q,)),
                dma((pieces, CHUNKS)),
                dma,
                dma((3,)),
                dma((3,)),
                dma((3,)),
                dma((3,)),
                dma,
                dma,
                dma,
                dma,
            ],
            compiler_params=pltpu.CompilerParams(
                collective_id=0, has_side_effects=True, vmem_limit_bytes=56 << 20
            ),
        )(acts[0, 0], output_gradient[0], gains, down[0], up[0], thresholds[0], lengths, owners)
        return ig[None, None], lora[None], owned[None]

    placed = (
        P("section", None, "dp", None),
        P(None, "dp", None),
        P("section", None),
        P("section", None, None),
        P("section", None, None),
        P("section", None, None),
        P(),
        P(),
    )
    return jax.shard_map(
        on_device,
        mesh=mesh,
        in_specs=placed,
        out_specs=(P("section", None, "dp", None), P("section", "dp", None), P("section", None, "dp")),
        check_vma=False,
    )
```

```python
import functools

import jax
import jax.numpy as jnp
from jax import lax
from jax.experimental import pallas as pl
from jax.experimental.pallas import tpu as pltpu
from jax.sharding import PartitionSpec as P

OWN = 8
NORM_EPS = 1e-06
MESH = pl.DeviceIdType.MESH
F32, BF16 = jnp.float32, jnp.bfloat16
R = 4
Q = 4
L = 8
G = 16
LANE = 128
CHUNKS = 3
PASSED, AWAY = 3, 12
PASS_GROUPS = 5
ORDER = (4, 3, 5, 2, 6, 1, 7, 0)
LATE = 1


def dot(a, b):
    return jnp.dot(a, b, preferred_element_type=F32)


def dot_nt(a, b):
    return lax.dot_general(a, b, (((1,), (1,)), ((), ())), preferred_element_type=F32)


def pick(top, bottom):
    row = lax.broadcasted_iota(jnp.int32, top.shape, 0)
    return jnp.where(row < R, top, bottom)


def turn(v):
    return pltpu.roll(v, R, 0)


def pack(v, width):
    a, b, c, d = [v[:, q * width:(q + 1) * width] for q in range(Q)]
    first = jnp.concatenate([pick(a, turn(b)), pick(c, turn(d))], axis=0)
    second = jnp.concatenate([pick(turn(a), b), pick(turn(c), d)], axis=0)
    return first.astype(BF16), second.astype(BF16)


def unpack(first, second):
    first, second = first.astype(F32), second.astype(F32)
    out = []
    for h in range(Q // 2):
        a, b = first[h * L:(h + 1) * L], second[h * L:(h + 1) * L]
        out += [pick(a, turn(b)), pick(turn(a), b)]
    return out


def doubled(v):
    w = turn(v)
    return pick(v, w), pick(w, v)


def fold(both):
    t = [both[(q // 2) * L:(q // 2 + 1) * L, q * LANE:(q + 1) * LANE] for q in range(Q)]
    y = pick(t[0], t[1]) + pick(t[2], t[3])
    return y + turn(y)


def widen(low):
    zero = jnp.zeros_like(low)
    upper, lower = pick(low, zero), pick(zero, low)
    return jnp.concatenate([
        jnp.concatenate([upper, lower, zero, zero], axis=1),
        jnp.concatenate([zero, zero, upper, lower], axis=1),
    ], axis=0).astype(BF16)


def kernel(n_sec, n_dp, *refs):
    (acts, og, gains, dn, up, thr, lens, own, ig, lora, owned,
     xv, flat, ucat, dv, dtc, normed, xp, arr, outp, scale, hidf, hidb, hidp, lowp, stage, passing_by,
     r_n, r_a, r_h, nw, hw, parts, part_f, other, hid_t, low_t, doc_row, doc_col,
     s_load, s_chain, c_send, rs, rso, ss, sso, p_send, p_recv, o_send, o_recv, by_send, by_recv) = refs
    tok, feat = xv.shape
    width = feat // Q
    n_docs = lens.shape[1]
    pieces, groups = tok // R, tok // G
    n_z = n_dp // 2
    per_chip = feat // n_z
    win = r_n.shape[1]
    blocks = n_dp // 2
    span = blocks * tok
    cols = tok + tok // 2
    lanes = width // CHUNKS

    sec = lax.axis_index("section")
    me = lax.axis_index("dp")
    z, core = me // 2, lax.rem(me, 2)
    side = me // blocks
    slot = lax.rem(me, blocks)
    last = n_sec - 1
    first_half = core == 0

    def load(src, dst, i):
        return pltpu.make_async_copy(src, dst, s_load.at[i])

    loads = [load(dn, dv, 0), load(acts, xv, 1)] + [
        load(up.at[pl.ds(q * width, width)], ucat.at[:, pl.ds(q * LANE, LANE)], 2 + q) for q in range(Q)
    ]
    for c in loads:
        c.start()

    @pl.when(sec == last)
    def _():
        load(og, flat, 2 + Q).start()

    barrier = pltpu.get_barrier_semaphore()

    def greet(who):
        pl.semaphore_signal(barrier, inc=1, device_id=who, device_id_type=MESH)

    @pl.when(sec > 0)
    def _():
        greet({"section": sec - 1})

    @pl.when(sec < last)
    def _():
        greet({"section": sec + 1})

    for peer in range(n_dp):
        @pl.when(me != peer)
        def _():
            greet({"dp": peer})

    opposite = lax.rem(z + n_z // 2, n_z)
    passed = sec < PASSED
    passing = (sec >= AWAY) & (sec < AWAY + PASSED)

    @pl.when(passing)
    def _():
        greet({"section": sec - AWAY})

    @pl.when(passed & (core == opposite * 2 // n_z))
    def _():
        for c in range(2):
            greet({"section": sec + AWAY, "dp": 2 * opposite + c})

    @pl.when(core == 1)
    def _():
        for r in (r_n, r_a, r_h):
            r[pl.ds(span, tok // 2), :] = jnp.zeros((tok // 2, r.shape[1]), BF16)

    loads[0].wait()

    def turn_map(t, _):
        here = pl.ds(pl.multiple_of(t * LANE, LANE), LANE)
        for q in range(Q):
            there = pl.ds(pl.multiple_of(t * LANE + q * width, LANE), LANE)
            dtc[pl.ds(q * LANE, LANE), here] = (dv[there, :].astype(F32).T * gains[:, there]).astype(BF16)
        return 0

    lax.fori_loop(0, width // LANE, turn_map, 0)
    loads[1].wait()

    def norm_group(q, _):
        rows = pl.ds(pl.multiple_of(q * G, G), G)
        v = xv[rows, :].astype(F32)
        s = lax.rsqrt(jnp.sum(v * v, axis=1, keepdims=True) / feat + NORM_EPS)
        normed[rows, :] = (v * s * gains[...]).astype(BF16)
        for h in range(G // L):
            p = q * (G // R) + 2 * h
            own_rows = slice(h * L, (h + 1) * L)
            xp[p], xp[p + 1] = pack(v[own_rows], width)
            scale[p], scale[p + 1] = doubled(jnp.broadcast_to(s[own_rows], (L, LANE)))
        return 0

    lax.fori_loop(0, groups, norm_group, 0)
    hidf[...] = jnp.zeros_like(hidf)

    def down_part(t, _):
        here = pl.ds(pl.multiple_of(t * (width // 3), LANE), width // 3)
        hidf[...] += dot(normed[:, here], dv[here, :])
        return 0

    lax.fori_loop(0, 3 * Q, down_part, 0)
    hidb[...] = hidf[...].astype(BF16)
    for h in range(tok // L):
        hidp[2 * h], hidp[2 * h + 1] = doubled(hidf[pl.ds(h * L, L), :])

    @pl.when(sec == last)
    def _():
        load(og, flat, 2 + Q).wait()

        def pack_group(q, _):
            rows = pl.ds(pl.multiple_of(q * G, G), G)
            v = flat[rows, :].astype(F32)
            for h in range(G // L):
                p = q * (G // R) + 2 * h
                arr[p], arr[p + 1] = pack(v[h * L:(h + 1) * L], width)
            return 0

        lax.fori_loop(0, groups, pack_group, 0)

    for c in loads[2:]:
        c.wait()
    ends = jnp.where(sec > 0, 1, 0) + jnp.where(sec < last, 1, 0)
    extra = jnp.where(passed | passing, 1, 0)
    pl.semaphore_wait(barrier, n_dp - 1 + ends + extra)

    def send(src, dst, i, zz, dest_core, row, n, sems, other_chip):
        d = dst.at[pl.ds(pl.multiple_of(row, G), n), :]
        dest = 2 * zz + dest_core

        def remote():
            pltpu.make_async_remote_copy(
                src_ref=src, dst_ref=d, send_sem=sems[0].at[i], recv_sem=sems[1].at[i],
                device_id={"dp": dest}, device_id_type=MESH,
            ).start()

        if other_chip is True:
            remote()
            return

        @pl.when(dest == me)
        def _():
            pltpu.make_async_copy(src, d, sems[1].at[i]).start()

        @pl.when(dest != me)
        def _():
            remote()

    def spread_own(turn_of):
        zz = lax.rem(z + turn_of, n_z)
        start = pl.multiple_of(per_chip * zz // LANE * LANE, LANE)
        there = pl.ds(start, win)
        send(normed.at[:, there], r_n, 0, zz, side, slot * tok, tok, (ss, rs), None)
        send(hidb, r_h, 1, zz, side, slot * tok, tok, (ss, rs), None)

        @pl.when(me == blocks)
        def _():
            top = pl.ds(0, tok // 2)
            send(normed.at[top, there], r_n, 0, zz, 0, span, tok // 2, (sso, rso), None)
            send(hidb.at[top], r_h, 1, zz, 0, span, tok // 2, (sso, rso), None)

    def spread_all(zz, _):
        spread_own(zz)
        return 0

    def whole_rows(src, q):
        p = q * (G // R)
        both = [unpack(src[p + 2 * h], src[p + 2 * h + 1]) for h in range(G // L)]
        return [jnp.concatenate(x, axis=0) for x in zip(*both)]

    def spread_arriving(q):
        row = q * G
        quarters = whole_rows(arr, q)
        p = q * (G // R)
        low = jnp.concatenate(
            [pick(lowp[p + 2 * h], lowp[p + 2 * h + 1]) for h in range(G // L)], axis=0).astype(BF16)
        lane = lax.broadcasted_iota(jnp.int32, (1, LANE), 1)
        for zz in range(n_z):
            first = per_chip * zz
            start = first // LANE * LANE
            part = start // width
            l0 = start - part * width
            w = quarters[part][:, l0:l0 + win]
            w = jnp.concatenate([
                w[:, :LANE] * jnp.where(lane >= first - start, 1.0, 0.0),
                w[:, LANE:win - LANE],
                w[:, win - LANE:] * jnp.where(lane < first + per_chip - (start + win - LANE), 1.0, 0.0),
            ], axis=1)
            stage[q, zz, :, pl.ds(0, win)] = w.astype(BF16)
            stage[q, zz, :, pl.ds(win, LANE)] = low
        for k in ORDER:
            zz = lax.rem(z + k, n_z)
            src = stage.at[q, zz]
            if 2 * k == n_z:
                direct = jnp.logical_not(passed & (q < PASS_GROUPS))

                @pl.when(direct)
                def _():
                    send(src, r_a, 2, zz, side, slot * tok + row, G, (ss, rs), True)

                @pl.when(jnp.logical_not(direct))
                def _():
                    pltpu.make_async_remote_copy(
                        src_ref=src, dst_ref=passing_by.at[q], send_sem=ss.at[2], recv_sem=by_recv.at[q],
                        device_id={"section": sec + AWAY}, device_id_type=MESH,
                    ).start()
            else:
                send(src, r_a, 2, zz, side, slot * tok + row, G, (ss, rs), k != 0)

            @pl.when((me == blocks) & (row < tok // 2))
            def _():
                send(src, r_a, 2, zz, 0, span + lax.rem(row, tok // 2), G, (sso, rso), k != 0)

    def doc_tables():
        k_row = lax.broadcasted_iota(jnp.int32, (n_docs, n_docs), 1)
        k_col = lax.broadcasted_iota(jnp.int32, (n_docs, n_docs), 0)
        len_row = lens[...].astype(F32)
        len_col = jnp.sum(jnp.where(k_row == k_col, len_row, 0.0), axis=1, keepdims=True)
        ends_col = jnp.sum(jnp.where(k_row <= k_col, len_row, 0.0), axis=1, keepdims=True)
        ends_row = jnp.sum(jnp.where(k_col <= k_row, len_col, 0.0), axis=0, keepdims=True)
        base = core * span

        def at(b, _):
            start = pl.multiple_of(b * tok, tok)
            pos_r = (lax.broadcasted_iota(jnp.int32, (n_docs, tok), 1) + (base + start)).astype(F32)
            doc_row[:, pl.ds(start, tok)] = jnp.broadcast_to(
                jnp.sum(jnp.where(ends_col <= pos_r, 1.0, 0.0), axis=0, keepdims=True), (8, tok))
            pos_c = (lax.broadcasted_iota(jnp.int32, (tok, n_docs), 0) + (base + start)).astype(F32)
            doc_col[pl.ds(start, tok), :] = jnp.broadcast_to(
                jnp.sum(jnp.where(ends_row <= pos_c, 1.0, 0.0), axis=1, keepdims=True), (tok, LANE))
            return 0

        lax.fori_loop(0, blocks + 1, at, 0)

    early = sec < n_sec - LATE

    @pl.when(early)
    def _():
        lax.fori_loop(0, n_z, spread_all, 0)

    def chain_copy(p, c):
        there = pl.ds(c * lanes, lanes)
        return pltpu.make_async_remote_copy(
            src_ref=outp.at[p, :, there], dst_ref=arr.at[p, :, there],
            send_sem=c_send, recv_sem=s_chain.at[p, c],
            device_id={"section": jnp.maximum(sec - 1, 0)}, device_id_type=MESH,
        )

    parts_of = [pl.ds(c * lanes, lanes) for c in range(CHUNKS)]

    def piece(p, recv, send_on):
        both = jnp.zeros((2 * L, Q * LANE), F32)
        for c, there in enumerate(parts_of):
            if recv:
                chain_copy(p, c).wait_recv()
            both += dot(arr[p, :, there], ucat[there, :])
        low = fold(both).astype(BF16).astype(F32)
        s = scale[p][:, :1]
        k = s * s * (jnp.sum(low * hidp[p], axis=1, keepdims=True) / feat)
        s2, k2 = jnp.concatenate([s, s], axis=0), jnp.concatenate([k, k], axis=0)
        wide = widen(low)
        for c, there in enumerate(parts_of):
            out = arr[p, :, there].astype(F32) + s2 * dot(wide, dtc[:, there]) - k2 * xp[p, :, there].astype(F32)
            outp[p, :, there] = out.astype(BF16)
            if send_on:
                chain_copy(p, c).start()
        lowp[p] = low

    def group(q, kind):
        for t in range(G // R):
            piece(q * (G // R) + t, *kind)
        spread_arriving(q)

        @pl.when(jnp.logical_not(early))
        def _():
            spread_own(q)

        rows = pl.ds(pl.multiple_of(q * G, G), G)
        for part, v in enumerate(whole_rows(outp, q)):
            ig[rows, pl.ds(part * width, width)] = v.astype(BF16)

    def run(where, *kind):
        @pl.when(where)
        def _():
            def step(q, _):
                group(q, kind)
                return 0

            lax.fori_loop(0, groups, step, 0)

    run(sec == last, False, True)
    run((sec > 0) & (sec < last), True, True)
    run(sec == 0, True, False)

    def arrived(dst, i):
        pltpu.make_async_copy(dst.at[pl.ds(0, span)], dst.at[pl.ds(0, span)], rs.at[i]).wait()

        @pl.when(first_half)
        def _():
            over = dst.at[pl.ds(span, tok // 2)]
            pltpu.make_async_copy(over, over, rso.at[i]).wait()

    doc_tables()
    arrived(r_n, 0)
    arrived(r_h, 1)
    offset = lax.rem(z, 2) * (LANE // 2)
    lane = lax.broadcasted_iota(jnp.int32, (1, win), 1)
    inside = jnp.where((lane >= offset) & (lane < offset + per_chip), 1.0, 0.0)
    column = jnp.where(lax.broadcasted_iota(jnp.int32, (1, cols), 1) < tok, 1.0, 2.0)

    def mine(src, b):
        return (src[pl.ds(b * tok, tok), :].astype(F32) * inside).astype(BF16)

    for b in range(blocks):
        there = pl.ds(b * tok, cols)
        same = doc_col[pl.ds(b * tok, tok), :1] == doc_row[:1, there]
        weight = jnp.where(same, column, 0.0)
        nw[b] = weight * dot_nt(mine(r_n, b), r_n[there, :])
        hw[b] = weight * dot_nt(r_h[pl.ds(b * tok, tok), :], r_h[there, :])
        hid_t[:, pl.ds(b * tok, tok)] = r_h[pl.ds(b * tok, tok), :].astype(F32).T

    @pl.when(passing)
    def _():
        def pass_on(q, _):
            block = passing_by.at[q]
            pltpu.make_async_copy(block, block, by_recv.at[q]).wait()
            at = pl.multiple_of(slot * tok + q * G, G)
            pltpu.make_async_remote_copy(
                src_ref=block, dst_ref=r_a.at[pl.ds(at, G), :], send_sem=by_send, recv_sem=rs.at[2],
                device_id={"section": sec - AWAY, "dp": 2 * opposite + side}, device_id_type=MESH,
            ).start()
            return 0

        lax.fori_loop(0, PASS_GROUPS, pass_on, 0)

    arrived(r_a, 2)
    win_l, low_l = pl.ds(0, win), pl.ds(win, LANE)
    total = jnp.zeros((1, LANE), F32)
    doc_lane = lax.broadcasted_iota(jnp.int32, (tok, LANE), 1).astype(F32)
    for b in range(blocks):
        there, here = pl.ds(b * tok, cols), pl.ds(b * tok, tok)
        pair = nw[b] * dot_nt(r_a[here, low_l], r_a[there, low_l]) + hw[b] * dot_nt(r_a[here, win_l], r_a[there, win_l])
        row_sum = jnp.sum(pair, axis=1, keepdims=True)
        total += jnp.sum(jnp.where(doc_col[here, :] == doc_lane, row_sum, 0.0), axis=0, keepdims=True)
    parts[me] = jnp.broadcast_to(total, (8, LANE))

    for peer in range(n_dp):
        @pl.when(me != peer)
        def _():
            pltpu.make_async_remote_copy(
                src_ref=parts.at[me], dst_ref=parts.at[me], send_sem=p_send, recv_sem=p_recv,
                device_id={"dp": peer}, device_id_type=MESH,
            ).start()

    for b in range(blocks):
        here = pl.ds(b * tok, tok)
        low_t[:, here] = r_a[here, low_l].astype(F32).T

    most = parts.at[pl.ds(0, n_dp - 1)]
    pltpu.make_async_copy(most, most, p_recv).wait()
    pair_sum = jnp.sum(parts[...], axis=0)[:1, :n_docs]
    ratio = jnp.sqrt(pair_sum / (feat * LANE) + NORM_EPS) / thr[...]
    clip = jnp.minimum(1.0, 1.0 / ratio)
    k_row = lax.broadcasted_iota(jnp.int32, (n_docs, n_docs), 1)
    k_col = lax.broadcasted_iota(jnp.int32, (n_docs, n_docs), 0)
    clip_col = jnp.sum(jnp.where(k_row == k_col, clip, 0.0), axis=1, keepdims=True)
    doc_id = lax.broadcasted_iota(jnp.int32, (n_docs, span), 0).astype(F32)
    token_clip = jnp.sum(
        jnp.where(doc_row[:1, pl.ds(0, span)] == doc_id, clip_col, 0.0), axis=0, keepdims=True)
    down = dot((low_t[...] * token_clip).astype(BF16), r_n[pl.ds(0, span), :])
    up_g = dot((hid_t[...] * token_clip).astype(BF16), r_a[pl.ds(0, span), win_l])
    part_f[:, pl.ds(0, LANE)] = down.T
    part_f[:, pl.ds(LANE, LANE)] = up_g.T
    own_rows = pl.multiple_of(offset + core * (per_chip // 2), 8)
    far_rows = pl.multiple_of(offset + (1 - core) * (per_chip // 2), 8)
    swap = pltpu.make_async_remote_copy(
        src_ref=part_f.at[pl.ds(far_rows, per_chip // 2)], dst_ref=other,
        send_sem=o_send, recv_sem=o_recv,
        device_id={"dp": 2 * z + (1 - core)}, device_id_type=MESH,
    )
    swap.start()

    own_row = jnp.where(own[...] == me, 1.0, 0.0)
    own_col = jnp.sum(jnp.where(k_row == k_col, own_row, 0.0), axis=1, keepdims=True)
    rank_col = jnp.sum(jnp.where(k_row <= k_col, own_row, 0.0), axis=1, keepdims=True) - 1.0
    ratio_col = jnp.sum(jnp.where(k_row == k_col, ratio, 0.0), axis=1, keepdims=True)
    slot_id = lax.broadcasted_iota(jnp.int32, (n_docs, OWN), 1).astype(F32)
    held = jnp.where((own_col > 0.5) & (rank_col == slot_id), ratio_col, 0.0)
    owned[...] = jnp.sum(held, axis=0, keepdims=True)

    swap.wait()
    lora[...] = (part_f[pl.ds(own_rows, per_chip // 2), :] + other[...]) / n_docs

    pltpu.make_async_copy(most, most, p_send).wait()

    @pl.when(sec > 0)
    def _():
        pltpu.make_async_copy(outp, outp, c_send).wait()

    @pl.when(passing)
    def _():
        some = passing_by.at[pl.ds(0, PASS_GROUPS)]
        pltpu.make_async_copy(some, some, by_send).wait()

    for i, dst in enumerate((r_n, r_h, r_a)):
        @pl.when(core == side)
        def _():
            whole = dst.at[pl.ds(0, (n_z - 1) * tok)]
            pltpu.make_async_copy(whole, whole, ss.at[i]).wait()

        @pl.when(core != side)
        def _():
            whole = dst.at[pl.ds(0, n_z * tok)]
            pltpu.make_async_copy(whole, whole, ss.at[i]).wait()

        @pl.when(me == blocks)
        def _():
            whole = dst.at[pl.ds(0, (n_z - 1) * (tok // 2))]
            pltpu.make_async_copy(whole, whole, sso.at[i]).wait()


def solution(mesh):
    n_sec, n_dp = mesh.shape["section"], mesh.shape["dp"]
    n_z = n_dp // 2

    def on_device(acts, output_gradient, gains, down, up, thresholds, lengths, owners):
        tok, feat = acts.shape[2:]
        rank = down.shape[2]
        width = feat // Q
        per_chip = feat // n_z
        win = -(-per_chip // LANE) * LANE
        pieces, blocks = tok // R, n_dp // 2
        span = blocks * tok
        long = span + tok // 2
        cols = tok + tok // 2
        hbm = pl.BlockSpec(memory_space=pl.ANY)
        vmem = pl.BlockSpec(memory_space=pltpu.VMEM)
        dma = pltpu.SemaphoreType.DMA
        packed = pltpu.VMEM((pieces, Q * R, width), BF16)
        whole = pltpu.VMEM((tok, feat), BF16)
        ig, lora, owned = pl.pallas_call(
            functools.partial(kernel, n_sec, n_dp),
            out_shape=(
                pltpu.VMEM((tok, feat), BF16),
                pltpu.VMEM((feat // n_dp, 2 * rank), F32),
                pltpu.VMEM((1, OWN), F32),
            ),
            in_specs=[hbm, hbm, vmem, hbm, hbm, vmem, vmem, vmem],
            out_specs=(vmem, vmem, vmem),
            scratch_shapes=[
                whole,
                whole,
                pltpu.VMEM((width, Q * rank), BF16),
                pltpu.VMEM((feat, rank), BF16),
                pltpu.VMEM((Q * rank, width), BF16),
                whole,
                packed,
                packed,
                packed,
                pltpu.VMEM((pieces, L, LANE), F32),
                pltpu.VMEM((tok, rank), F32),
                pltpu.VMEM((tok, rank), BF16),
                pltpu.VMEM((pieces, L, rank), F32),
                pltpu.VMEM((pieces, L, rank), F32),
                pltpu.VMEM((tok // G, n_z, G, win + rank), BF16),
                pltpu.VMEM((tok // G, G, win + rank), BF16),
                pltpu.VMEM((long, win), BF16),
                pltpu.VMEM((long, win + rank), BF16),
                pltpu.VMEM((long, rank), BF16),
                pltpu.VMEM((blocks, tok, cols), F32),
                pltpu.VMEM((blocks, tok, cols), F32),
                pltpu.VMEM((n_dp, 8, LANE), F32),
                pltpu.VMEM((win, 2 * rank), F32),
                pltpu.VMEM((per_chip // 2, 2 * rank), F32),
                pltpu.VMEM((rank, span), F32),
                pltpu.VMEM((rank, span), F32),
                pltpu.VMEM((8, span + tok), F32),
                pltpu.VMEM((span + tok, LANE), F32),
                dma((3 + Q,)),
                dma((pieces, CHUNKS)),
                dma,
                dma((3,)),
                dma((3,)),
                dma((3,)),
                dma((3,)),
                dma,
                dma,
                dma,
                dma,
                dma,
                dma((tok // G,)),
            ],
            compiler_params=pltpu.CompilerParams(
                collective_id=0, has_side_effects=True, vmem_limit_bytes=56 << 20
            ),
        )(acts[0, 0], output_gradient[0], gains, down[0], up[0], thresholds[0], lengths, owners)
        return ig[None, None], lora[None], owned[None]

    placed = (
        P("section", None, "dp", None),
        P(None, "dp", None),
        P("section", None),
        P("section", None, None),
        P("section", None, None),
        P("section", None, None),
        P(),
        P(),
    )
    return jax.shard_map(
        on_device,
        mesh=mesh,
        in_specs=placed,
        out_specs=(P("section", None, "dp", None), P("section", "dp", None), P("section", None, "dp")),
        check_vma=False,
    )
```

```python
import functools

import jax
import jax.numpy as jnp
from jax import lax
from jax.experimental import pallas as pl
from jax.experimental.pallas import tpu as pltpu
from jax.sharding import PartitionSpec as P

OWN = 8
NORM_EPS = 1e-06
MESH = pl.DeviceIdType.MESH
F32, BF16 = jnp.float32, jnp.bfloat16
R = 4
Q = 4
L = 8
G = 16
LANE = 128
CHUNKS = 3
PASSED, AWAY = 3, 12
PASS_GROUPS = 5
ORDER = (4, 3, 5, 2, 6, 1, 7, 0)
LATE = 1


def dot(a, b):
    return jnp.dot(a, b, preferred_element_type=F32)


def dot_nt(a, b):
    return lax.dot_general(a, b, (((1,), (1,)), ((), ())), preferred_element_type=F32)


def pick(top, bottom):
    row = lax.broadcasted_iota(jnp.int32, top.shape, 0)
    return jnp.where(row < R, top, bottom)


def turn(v):
    return pltpu.roll(v, R, 0)


def pack(v, width):
    a, b, c, d = [v[:, q * width:(q + 1) * width] for q in range(Q)]
    first = jnp.concatenate([pick(a, turn(b)), pick(c, turn(d))], axis=0)
    second = jnp.concatenate([pick(turn(a), b), pick(turn(c), d)], axis=0)
    return first.astype(BF16), second.astype(BF16)


def unpack(first, second):
    first, second = first.astype(F32), second.astype(F32)
    out = []
    for h in range(Q // 2):
        a, b = first[h * L:(h + 1) * L], second[h * L:(h + 1) * L]
        out += [pick(a, turn(b)), pick(turn(a), b)]
    return out


def doubled(v):
    w = turn(v)
    return pick(v, w), pick(w, v)


def fold(both):
    t = [both[(q // 2) * L:(q // 2 + 1) * L, q * LANE:(q + 1) * LANE] for q in range(Q)]
    y = pick(t[0], t[1]) + pick(t[2], t[3])
    return y + turn(y)


def widen(low):
    zero = jnp.zeros_like(low)
    upper, lower = pick(low, zero), pick(zero, low)
    return jnp.concatenate([
        jnp.concatenate([upper, lower, zero, zero], axis=1),
        jnp.concatenate([zero, zero, upper, lower], axis=1),
    ], axis=0).astype(BF16)


def kernel(n_sec, n_dp, *refs):
    (acts, og, gains, dn, up, thr, lens, own, ig, lora, owned,
     xv, flat, ucat, dv, dtc, normed, xp, arr, outp, scale, hidf, hidb, hidp, lowp, stage, passing_by,
     r_n, r_a, r_h, nw, hw, parts, part_f, other, hid_t, low_t, doc_row, doc_col,
     s_load, s_chain, c_send, rs, rso, ss, sso, p_send, p_recv, o_send, o_recv, by_send, by_recv) = refs
    tok, feat = xv.shape
    width = feat // Q
    n_docs = lens.shape[1]
    pieces, groups = tok // R, tok // G
    n_z = n_dp // 2
    per_chip = feat // n_z
    win = r_n.shape[1]
    blocks = n_dp // 2
    span = blocks * tok
    cols = tok + tok // 2
    lanes = width // CHUNKS

    sec = lax.axis_index("section")
    me = lax.axis_index("dp")
    z, core = me // 2, lax.rem(me, 2)
    side = me // blocks
    slot = lax.rem(me, blocks)
    last = n_sec - 1
    first_half = core == 0

    def load(src, dst, i):
        return pltpu.make_async_copy(src, dst, s_load.at[i])

    loads = [load(dn, dv, 0), load(acts, xv, 1)] + [
        load(up.at[pl.ds(q * width, width)], ucat.at[:, pl.ds(q * LANE, LANE)], 2 + q) for q in range(Q)
    ]
    for c in loads:
        c.start()

    @pl.when(sec == last)
    def _():
        load(og, flat, 2 + Q).start()

    barrier = pltpu.get_barrier_semaphore()

    def greet(who):
        pl.semaphore_signal(barrier, inc=1, device_id=who, device_id_type=MESH)

    @pl.when(sec > 0)
    def _():
        greet({"section": sec - 1})

    @pl.when(sec < last)
    def _():
        greet({"section": sec + 1})

    for peer in range(n_dp):
        @pl.when(me != peer)
        def _():
            greet({"dp": peer})

    opposite = lax.rem(z + n_z // 2, n_z)
    passed = sec < PASSED
    passing = (sec >= AWAY) & (sec < AWAY + PASSED)

    @pl.when(passing)
    def _():
        greet({"section": sec - AWAY})

    @pl.when(passed & (core == opposite * 2 // n_z))
    def _():
        for c in range(2):
            greet({"section": sec + AWAY, "dp": 2 * opposite + c})

    @pl.when(core == 1)
    def _():
        for r in (r_n, r_a, r_h):
            r[pl.ds(span, tok // 2), :] = jnp.zeros((tok // 2, r.shape[1]), BF16)

    loads[0].wait()

    def turn_map(t, _):
        here = pl.ds(pl.multiple_of(t * LANE, LANE), LANE)
        for q in range(Q):
            there = pl.ds(pl.multiple_of(t * LANE + q * width, LANE), LANE)
            dtc[pl.ds(q * LANE, LANE), here] = (dv[there, :].astype(F32).T * gains[:, there]).astype(BF16)
        return 0

    lax.fori_loop(0, width // LANE, turn_map, 0)
    loads[1].wait()

    def norm_group(q, _):
        rows = pl.ds(pl.multiple_of(q * G, G), G)
        v = xv[rows, :].astype(F32)
        s = lax.rsqrt(jnp.sum(v * v, axis=1, keepdims=True) / feat + NORM_EPS)
        normed[rows, :] = (v * s * gains[...]).astype(BF16)
        for h in range(G // L):
            p = q * (G // R) + 2 * h
            own_rows = slice(h * L, (h + 1) * L)
            xp[p], xp[p + 1] = pack(v[own_rows], width)
            scale[p], scale[p + 1] = doubled(jnp.broadcast_to(s[own_rows], (L, LANE)))
        return 0

    lax.fori_loop(0, groups, norm_group, 0)
    hidf[...] = jnp.zeros_like(hidf)

    def down_part(t, _):
        here = pl.ds(pl.multiple_of(t * (width // 3), LANE), width // 3)
        hidf[...] += dot(normed[:, here], dv[here, :])
        return 0

    lax.fori_loop(0, 3 * Q, down_part, 0)
    hidb[...] = hidf[...].astype(BF16)
    for h in range(tok // L):
        hidp[2 * h], hidp[2 * h + 1] = doubled(hidf[pl.ds(h * L, L), :])

    @pl.when(sec == last)
    def _():
        load(og, flat, 2 + Q).wait()

    def pack_group(q):
        rows = pl.ds(pl.multiple_of(q * G, G), G)
        v = flat[rows, :].astype(F32)
        for h in range(G // L):
            p = q * (G // R) + 2 * h
            arr[p], arr[p + 1] = pack(v[h * L:(h + 1) * L], width)

    for c in loads[2:]:
        c.wait()
    ends = jnp.where(sec > 0, 1, 0) + jnp.where(sec < last, 1, 0)
    extra = jnp.where(passed | passing, 1, 0)
    pl.semaphore_wait(barrier, n_dp - 1 + ends + extra)

    def send(src, dst, i, zz, dest_core, row, n, sems, other_chip):
        d = dst.at[pl.ds(pl.multiple_of(row, G), n), :]
        dest = 2 * zz + dest_core

        def remote():
            pltpu.make_async_remote_copy(
                src_ref=src, dst_ref=d, send_sem=sems[0].at[i], recv_sem=sems[1].at[i],
                device_id={"dp": dest}, device_id_type=MESH,
            ).start()

        if other_chip is True:
            remote()
            return

        @pl.when(dest == me)
        def _():
            pltpu.make_async_copy(src, d, sems[1].at[i]).start()

        @pl.when(dest != me)
        def _():
            remote()

    def spread_own(turn_of):
        zz = lax.rem(z + turn_of, n_z)
        start = pl.multiple_of(per_chip * zz // LANE * LANE, LANE)
        there = pl.ds(start, win)
        send(normed.at[:, there], r_n, 0, zz, side, slot * tok, tok, (ss, rs), None)
        send(hidb, r_h, 1, zz, side, slot * tok, tok, (ss, rs), None)

        @pl.when(me == blocks)
        def _():
            top = pl.ds(0, tok // 2)
            send(normed.at[top, there], r_n, 0, zz, 0, span, tok // 2, (sso, rso), None)
            send(hidb.at[top], r_h, 1, zz, 0, span, tok // 2, (sso, rso), None)

    def spread_all(zz, _):
        spread_own(zz)
        return 0

    def whole_rows(src, q):
        p = q * (G // R)
        both = [unpack(src[p + 2 * h], src[p + 2 * h + 1]) for h in range(G // L)]
        return [jnp.concatenate(x, axis=0) for x in zip(*both)]

    def spread_arriving(q):
        row = q * G
        quarters = whole_rows(arr, q)
        p = q * (G // R)
        low = jnp.concatenate(
            [pick(lowp[p + 2 * h], lowp[p + 2 * h + 1]) for h in range(G // L)], axis=0).astype(BF16)
        lane = lax.broadcasted_iota(jnp.int32, (1, LANE), 1)
        for zz in range(n_z):
            first = per_chip * zz
            start = first // LANE * LANE
            part = start // width
            l0 = start - part * width
            w = quarters[part][:, l0:l0 + win]
            w = jnp.concatenate([
                w[:, :LANE] * jnp.where(lane >= first - start, 1.0, 0.0),
                w[:, LANE:win - LANE],
                w[:, win - LANE:] * jnp.where(lane < first + per_chip - (start + win - LANE), 1.0, 0.0),
            ], axis=1)
            stage[q, zz, :, pl.ds(0, win)] = w.astype(BF16)
            stage[q, zz, :, pl.ds(win, LANE)] = low
        for k in ORDER:
            zz = lax.rem(z + k, n_z)
            src = stage.at[q, zz]
            if 2 * k == n_z:
                direct = jnp.logical_not(passed & (q < PASS_GROUPS))

                @pl.when(direct)
                def _():
                    send(src, r_a, 2, zz, side, slot * tok + row, G, (ss, rs), True)

                @pl.when(jnp.logical_not(direct))
                def _():
                    pltpu.make_async_remote_copy(
                        src_ref=src, dst_ref=passing_by.at[q], send_sem=ss.at[2], recv_sem=by_recv.at[q],
                        device_id={"section": sec + AWAY}, device_id_type=MESH,
                    ).start()
            else:
                send(src, r_a, 2, zz, side, slot * tok + row, G, (ss, rs), k != 0)

            @pl.when((me == blocks) & (row < tok // 2))
            def _():
                send(src, r_a, 2, zz, 0, span + lax.rem(row, tok // 2), G, (sso, rso), k != 0)

    def doc_tables():
        k_row = lax.broadcasted_iota(jnp.int32, (n_docs, n_docs), 1)
        k_col = lax.broadcasted_iota(jnp.int32, (n_docs, n_docs), 0)
        len_row = lens[...].astype(F32)
        len_col = jnp.sum(jnp.where(k_row == k_col, len_row, 0.0), axis=1, keepdims=True)
        ends_col = jnp.sum(jnp.where(k_row <= k_col, len_row, 0.0), axis=1, keepdims=True)
        ends_row = jnp.sum(jnp.where(k_col <= k_row, len_col, 0.0), axis=0, keepdims=True)
        base = core * span

        def at(b, _):
            start = pl.multiple_of(b * tok, tok)
            pos_r = (lax.broadcasted_iota(jnp.int32, (n_docs, tok), 1) + (base + start)).astype(F32)
            doc_row[:, pl.ds(start, tok)] = jnp.broadcast_to(
                jnp.sum(jnp.where(ends_col <= pos_r, 1.0, 0.0), axis=0, keepdims=True), (8, tok))
            pos_c = (lax.broadcasted_iota(jnp.int32, (tok, n_docs), 0) + (base + start)).astype(F32)
            doc_col[pl.ds(start, tok), :] = jnp.broadcast_to(
                jnp.sum(jnp.where(ends_row <= pos_c, 1.0, 0.0), axis=1, keepdims=True), (tok, LANE))
            return 0

        lax.fori_loop(0, blocks + 1, at, 0)

    early = sec < n_sec - LATE

    @pl.when(early)
    def _():
        lax.fori_loop(0, n_z, spread_all, 0)

    def chain_copy(p, c):
        there = pl.ds(c * lanes, lanes)
        return pltpu.make_async_remote_copy(
            src_ref=outp.at[p, :, there], dst_ref=arr.at[p, :, there],
            send_sem=c_send, recv_sem=s_chain.at[p, c],
            device_id={"section": jnp.maximum(sec - 1, 0)}, device_id_type=MESH,
        )

    parts_of = [pl.ds(c * lanes, lanes) for c in range(CHUNKS)]

    def piece(p, recv, send_on):
        both = jnp.zeros((2 * L, Q * LANE), F32)
        for c, there in enumerate(parts_of):
            if recv:
                chain_copy(p, c).wait_recv()
            both += dot(arr[p, :, there], ucat[there, :])
        low = fold(both).astype(BF16).astype(F32)
        s = scale[p][:, :1]
        k = s * s * (jnp.sum(low * hidp[p], axis=1, keepdims=True) / feat)
        s2, k2 = jnp.concatenate([s, s], axis=0), jnp.concatenate([k, k], axis=0)
        wide = widen(low)
        for c, there in enumerate(parts_of):
            out = arr[p, :, there].astype(F32) + s2 * dot(wide, dtc[:, there]) - k2 * xp[p, :, there].astype(F32)
            outp[p, :, there] = out.astype(BF16)
            if send_on:
                chain_copy(p, c).start()
        lowp[p] = low

    def group(q, kind):
        if not kind[0]:
            pack_group(q)
        for t in range(G // R):
            piece(q * (G // R) + t, *kind)
        spread_arriving(q)

        @pl.when(jnp.logical_not(early))
        def _():
            spread_own(q)

        rows = pl.ds(pl.multiple_of(q * G, G), G)
        for part, v in enumerate(whole_rows(outp, q)):
            ig[rows, pl.ds(part * width, width)] = v.astype(BF16)

    def run(where, *kind):
        @pl.when(where)
        def _():
            def step(q, _):
                group(q, kind)
                return 0

            lax.fori_loop(0, groups, step, 0)

    run(sec == last, False, True)
    run((sec > 0) & (sec < last), True, True)
    run(sec == 0, True, False)

    def arrived(dst, i):
        pltpu.make_async_copy(dst.at[pl.ds(0, span)], dst.at[pl.ds(0, span)], rs.at[i]).wait()

        @pl.when(first_half)
        def _():
            over = dst.at[pl.ds(span, tok // 2)]
            pltpu.make_async_copy(over, over, rso.at[i]).wait()

    doc_tables()
    arrived(r_n, 0)
    arrived(r_h, 1)
    offset = lax.rem(z, 2) * (LANE // 2)
    lane = lax.broadcasted_iota(jnp.int32, (1, win), 1)
    inside = jnp.where((lane >= offset) & (lane < offset + per_chip), 1.0, 0.0)
    column = jnp.where(lax.broadcasted_iota(jnp.int32, (1, cols), 1) < tok, 1.0, 2.0)

    def mine(src, b):
        return (src[pl.ds(b * tok, tok), :].astype(F32) * inside).astype(BF16)

    for b in range(blocks):
        there = pl.ds(b * tok, cols)
        same = doc_col[pl.ds(b * tok, tok), :1] == doc_row[:1, there]
        weight = jnp.where(same, column, 0.0)
        nw[b] = weight * dot_nt(mine(r_n, b), r_n[there, :])
        hw[b] = weight * dot_nt(r_h[pl.ds(b * tok, tok), :], r_h[there, :])
        hid_t[:, pl.ds(b * tok, tok)] = r_h[pl.ds(b * tok, tok), :].astype(F32).T

    @pl.when(passing)
    def _():
        def pass_on(q, _):
            block = passing_by.at[q]
            pltpu.make_async_copy(block, block, by_recv.at[q]).wait()
            at = pl.multiple_of(slot * tok + q * G, G)
            pltpu.make_async_remote_copy(
                src_ref=block, dst_ref=r_a.at[pl.ds(at, G), :], send_sem=by_send, recv_sem=rs.at[2],
                device_id={"section": sec - AWAY, "dp": 2 * opposite + side}, device_id_type=MESH,
            ).start()
            return 0

        lax.fori_loop(0, PASS_GROUPS, pass_on, 0)

    arrived(r_a, 2)
    win_l, low_l = pl.ds(0, win), pl.ds(win, LANE)
    total = jnp.zeros((1, LANE), F32)
    doc_lane = lax.broadcasted_iota(jnp.int32, (tok, LANE), 1).astype(F32)
    for b in range(blocks):
        there, here = pl.ds(b * tok, cols), pl.ds(b * tok, tok)
        pair = nw[b] * dot_nt(r_a[here, low_l], r_a[there, low_l]) + hw[b] * dot_nt(r_a[here, win_l], r_a[there, win_l])
        row_sum = jnp.sum(pair, axis=1, keepdims=True)
        total += jnp.sum(jnp.where(doc_col[here, :] == doc_lane, row_sum, 0.0), axis=0, keepdims=True)
    parts[me] = jnp.broadcast_to(total, (8, LANE))

    for peer in range(n_dp):
        @pl.when(me != peer)
        def _():
            pltpu.make_async_remote_copy(
                src_ref=parts.at[me], dst_ref=parts.at[me], send_sem=p_send, recv_sem=p_recv,
                device_id={"dp": peer}, device_id_type=MESH,
            ).start()

    for b in range(blocks):
        here = pl.ds(b * tok, tok)
        low_t[:, here] = r_a[here, low_l].astype(F32).T

    most = parts.at[pl.ds(0, n_dp - 1)]
    pltpu.make_async_copy(most, most, p_recv).wait()
    pair_sum = jnp.sum(parts[...], axis=0)[:1, :n_docs]
    ratio = jnp.sqrt(pair_sum / (feat * LANE) + NORM_EPS) / thr[...]
    clip = jnp.minimum(1.0, 1.0 / ratio)
    k_row = lax.broadcasted_iota(jnp.int32, (n_docs, n_docs), 1)
    k_col = lax.broadcasted_iota(jnp.int32, (n_docs, n_docs), 0)
    clip_col = jnp.sum(jnp.where(k_row == k_col, clip, 0.0), axis=1, keepdims=True)
    doc_id = lax.broadcasted_iota(jnp.int32, (n_docs, span), 0).astype(F32)
    token_clip = jnp.sum(
        jnp.where(doc_row[:1, pl.ds(0, span)] == doc_id, clip_col, 0.0), axis=0, keepdims=True)
    down = dot((low_t[...] * token_clip).astype(BF16), r_n[pl.ds(0, span), :])
    up_g = dot((hid_t[...] * token_clip).astype(BF16), r_a[pl.ds(0, span), win_l])
    part_f[:, pl.ds(0, LANE)] = down.T
    part_f[:, pl.ds(LANE, LANE)] = up_g.T
    own_rows = pl.multiple_of(offset + core * (per_chip // 2), 8)
    far_rows = pl.multiple_of(offset + (1 - core) * (per_chip // 2), 8)
    swap = pltpu.make_async_remote_copy(
        src_ref=part_f.at[pl.ds(far_rows, per_chip // 2)], dst_ref=other,
        send_sem=o_send, recv_sem=o_recv,
        device_id={"dp": 2 * z + (1 - core)}, device_id_type=MESH,
    )
    swap.start()

    own_row = jnp.where(own[...] == me, 1.0, 0.0)
    own_col = jnp.sum(jnp.where(k_row == k_col, own_row, 0.0), axis=1, keepdims=True)
    rank_col = jnp.sum(jnp.where(k_row <= k_col, own_row, 0.0), axis=1, keepdims=True) - 1.0
    ratio_col = jnp.sum(jnp.where(k_row == k_col, ratio, 0.0), axis=1, keepdims=True)
    slot_id = lax.broadcasted_iota(jnp.int32, (n_docs, OWN), 1).astype(F32)
    held = jnp.where((own_col > 0.5) & (rank_col == slot_id), ratio_col, 0.0)
    owned[...] = jnp.sum(held, axis=0, keepdims=True)

    swap.wait()
    lora[...] = (part_f[pl.ds(own_rows, per_chip // 2), :] + other[...]) / n_docs

    pltpu.make_async_copy(most, most, p_send).wait()

    @pl.when(sec > 0)
    def _():
        pltpu.make_async_copy(outp, outp, c_send).wait()

    @pl.when(passing)
    def _():
        some = passing_by.at[pl.ds(0, PASS_GROUPS)]
        pltpu.make_async_copy(some, some, by_send).wait()

    for i, dst in enumerate((r_n, r_h, r_a)):
        @pl.when(core == side)
        def _():
            whole = dst.at[pl.ds(0, (n_z - 1) * tok)]
            pltpu.make_async_copy(whole, whole, ss.at[i]).wait()

        @pl.when(core != side)
        def _():
            whole = dst.at[pl.ds(0, n_z * tok)]
            pltpu.make_async_copy(whole, whole, ss.at[i]).wait()

        @pl.when(me == blocks)
        def _():
            whole = dst.at[pl.ds(0, (n_z - 1) * (tok // 2))]
            pltpu.make_async_copy(whole, whole, sso.at[i]).wait()


def solution(mesh):
    n_sec, n_dp = mesh.shape["section"], mesh.shape["dp"]
    n_z = n_dp // 2

    def on_device(acts, output_gradient, gains, down, up, thresholds, lengths, owners):
        tok, feat = acts.shape[2:]
        rank = down.shape[2]
        width = feat // Q
        per_chip = feat // n_z
        win = -(-per_chip // LANE) * LANE
        pieces, blocks = tok // R, n_dp // 2
        span = blocks * tok
        long = span + tok // 2
        cols = tok + tok // 2
        hbm = pl.BlockSpec(memory_space=pl.ANY)
        vmem = pl.BlockSpec(memory_space=pltpu.VMEM)
        dma = pltpu.SemaphoreType.DMA
        packed = pltpu.VMEM((pieces, Q * R, width), BF16)
        whole = pltpu.VMEM((tok, feat), BF16)
        ig, lora, owned = pl.pallas_call(
            functools.partial(kernel, n_sec, n_dp),
            out_shape=(
                pltpu.VMEM((tok, feat), BF16),
                pltpu.VMEM((feat // n_dp, 2 * rank), F32),
                pltpu.VMEM((1, OWN), F32),
            ),
            in_specs=[hbm, hbm, vmem, hbm, hbm, vmem, vmem, vmem],
            out_specs=(vmem, vmem, vmem),
            scratch_shapes=[
                whole,
                whole,
                pltpu.VMEM((width, Q * rank), BF16),
                pltpu.VMEM((feat, rank), BF16),
                pltpu.VMEM((Q * rank, width), BF16),
                whole,
                packed,
                packed,
                packed,
                pltpu.VMEM((pieces, L, LANE), F32),
                pltpu.VMEM((tok, rank), F32),
                pltpu.VMEM((tok, rank), BF16),
                pltpu.VMEM((pieces, L, rank), F32),
                pltpu.VMEM((pieces, L, rank), F32),
                pltpu.VMEM((tok // G, n_z, G, win + rank), BF16),
                pltpu.VMEM((tok // G, G, win + rank), BF16),
                pltpu.VMEM((long, win), BF16),
                pltpu.VMEM((long, win + rank), BF16),
                pltpu.VMEM((long, rank), BF16),
                pltpu.VMEM((blocks, tok, cols), F32),
                pltpu.VMEM((blocks, tok, cols), F32),
                pltpu.VMEM((n_dp, 8, LANE), F32),
                pltpu.VMEM((win, 2 * rank), F32),
                pltpu.VMEM((per_chip // 2, 2 * rank), F32),
                pltpu.VMEM((rank, span), F32),
                pltpu.VMEM((rank, span), F32),
                pltpu.VMEM((8, span + tok), F32),
                pltpu.VMEM((span + tok, LANE), F32),
                dma((3 + Q,)),
                dma((pieces, CHUNKS)),
                dma,
                dma((3,)),
                dma((3,)),
                dma((3,)),
                dma((3,)),
                dma,
                dma,
                dma,
                dma,
                dma,
                dma((tok // G,)),
            ],
            compiler_params=pltpu.CompilerParams(
                collective_id=0, has_side_effects=True, vmem_limit_bytes=56 << 20
            ),
        )(acts[0, 0], output_gradient[0], gains, down[0], up[0], thresholds[0], lengths, owners)
        return ig[None, None], lora[None], owned[None]

    placed = (
        P("section", None, "dp", None),
        P(None, "dp", None),
        P("section", None),
        P("section", None, None),
        P("section", None, None),
        P("section", None, None),
        P(),
        P(),
    )
    return jax.shard_map(
        on_device,
        mesh=mesh,
        in_specs=placed,
        out_specs=(P("section", None, "dp", None), P("section", "dp", None), P("section", None, "dp")),
        check_vma=False,
    )
```
